512 devices in a mesh: wide: 128 (over y, z, x_hi), narrow: 4 (over x_lo, core).
Axes of the slice: x: 4 (x_hi: 2, x_lo: 2; x = x_hi * 2 + x_lo), y: 4, z: 16, core: 2. Of those that a mesh axis runs over, the one named last changes fastest.
Arguments:
- queries: bfloat16 [131072, 768], P(('wide', 'narrow')), may hold values from -8 to 8
- key_rows: bfloat16 [131072, 768], P(('wide', 'narrow')), may hold values from -8 to 8
- value_rows: bfloat16 [131072, 768], P(('wide', 'narrow')), may hold values from -6 to 6
- upstream: bfloat16 [131072, 768], P(('wide', 'narrow')), may hold values from -12 to 12
- pattern: int32 [1024, 11], P(('wide', 'narrow')), may hold values from 0 to 1, as said below
- expander_pick: int32 [512, 3], P(('wide', 'narrow')), may hold values from 0 to 1
Outputs:
- attention: bfloat16 [131072, 768], P(('wide', 'narrow'))
- query_grad: bfloat16 [131072, 768], P(('wide', 'narrow'))
- key_grad: bfloat16 [131072, 768], P(('wide', 'narrow'))
- value_grad: bfloat16 [131072, 768], P(('wide', 'narrow'))
The draws below stay inside these ranges and needn't reach their ends.
Inputs may be any that keep to these rules, and one draw needn't show every extreme that they name: `pattern`: row 2 * p + b belongs to block b of partition p and has a 1 in column b. Columns 2 and 3 hold a 1 in some row of every partition. Over the 2 rows of one partition at most 7 columns hold a 1, and in every draw some partition has exactly 7; partitions differ widely in how many.
All inputs are finite; a program needn't handle non-finite values.
Results may differ from the reference program's by a relative error of at most 0.033.
Values may be sent and summed in bfloat16 or wider, within the bound.
No kernel may reach another device: no remote copies, remote signals or barrier semaphores. Data moves between devices by JAX's collectives and lax.ppermute only.
A program may use at most 128 MiB of HBM per device.

```python
import jax
import jax.numpy as jnp
from jax import lax

D = 768
H = 12
HD = 64
BLK = 128
BW = 2
EXP = 3
CAND = 11
CMAX = 7
PARTS_SIZE = 512
NODES = 131072
N_WIDE = 128
N_NARROW = 4


def draw_queries(key, part):
    key = jax.random.fold_in(key, 21)
    drawn = 1.5 * jax.random.truncated_normal(key, -5.0, 5.0, (NODES, D), jnp.float32)
    return drawn.astype(jnp.bfloat16)


def draw_key_rows(key, part):
    key = jax.random.fold_in(key, 22)
    drawn = 1.5 * jax.random.truncated_normal(key, -5.0, 5.0, (NODES, D), jnp.float32)
    return drawn.astype(jnp.bfloat16)


def draw_pattern(key, part):
    key = jax.random.fold_in(key, 23)
    foreign = CAND - BW
    heat = jax.random.randint(jax.random.fold_in(key, 1), (PARTS_SIZE,), 0, 3)
    hottest = jax.random.randint(jax.random.fold_in(key, 2), (), 0, PARTS_SIZE)
    heat = jnp.where(jnp.arange(PARTS_SIZE) == hottest, 2, heat)
    reach = jnp.array([2, 3, CMAX - BW], jnp.int32)[heat]
    ranked = jax.random.randint(jax.random.fold_in(key, 3), (PARTS_SIZE, foreign), 0, 1 << 20) * foreign + jnp.arange(foreign)
    rim_first = jnp.arange(foreign) < 2
    ranked = jnp.where(rim_first[None, :], jnp.arange(foreign)[None, :] - 2, ranked)
    places = jnp.argsort(jnp.argsort(ranked, axis=1, stable=True), axis=1, stable=True)
    chosen = (places < reach[:, None]).astype(jnp.int32)
    chosen = jnp.concatenate([jnp.zeros((PARTS_SIZE, BW), jnp.int32), chosen], axis=1)[:, None, :]
    coins = jax.random.randint(jax.random.fold_in(key, 4), (PARTS_SIZE, BW, CAND), 0, 2)
    row_ids = jnp.arange(BW)[None, :, None]
    col_ids = jnp.arange(CAND)[None, None, :]
    own_part = jnp.where(col_ids < BW, jnp.where(col_ids == row_ids, 1, coins), 0)
    holder = (col_ids - BW) % BW == row_ids
    far_part = jnp.where(col_ids >= BW, chosen * jnp.where(holder, 1, coins), 0)
    return (own_part + far_part).reshape(PARTS_SIZE * BW, CAND).astype(jnp.int32)


def set_ends(result, key, smallest, top_value):
    shape = result.shape
    index_at = [jax.random.randint(jax.random.fold_in(key, axis), (), 0, shape[axis]) for axis in range(len(shape))]
    result = result.at[tuple(index_at)].set(smallest)
    longest = shape.index(max(shape))
    index_at[longest] = (index_at[longest] + 1) % shape[longest]
    return result.at[tuple(index_at)].set(top_value)


def shard_levels(key, extent, split, low, high):
    def one(position, blocks):
        steps = jax.random.uniform(jax.random.fold_in(jax.random.fold_in(key, 6), position), (blocks,), jnp.float32, low / len(split), high / len(split))
        return jnp.repeat(jnp.exp(steps), extent[position] // blocks).reshape((-1,) + (1,) * (len(extent) - position - 1))

    factor_of = one(*split[0])
    for cut in split[1:]:
        factor_of = factor_of * one(*cut)
    return factor_of


def scatter_about(stream_key, dims, deviation, bound, shards=(), kind=jnp.bfloat16):
    result = deviation * jax.random.normal(stream_key, dims, jnp.float32)
    if shards:
        result = result * shard_levels(stream_key, dims, shards, -0.22, 0.18)
    return jnp.clip(result, -bound, bound).astype(kind)


def setup_inputs(seed: int = 0) -> dict:
    streams_of = jax.random.split(jax.random.key(seed), 7)
    return {
        "queries": draw_queries(jax.random.fold_in(streams_of[6], 71), 0),
        "key_rows": draw_key_rows(jax.random.fold_in(streams_of[6], 71), 0),
        "value_rows": scatter_about(streams_of[2], (NODES, D), 1.0, 6.0, ((0, 512),)),
        "upstream": scatter_about(streams_of[3], (NODES, D), 2.0, 12.0, ((0, 512),)),
        "pattern": draw_pattern(jax.random.fold_in(streams_of[6], 71), 0),
        "expander_pick": set_ends(jax.random.randint(streams_of[5], (PARTS_SIZE, EXP), 0, BW), jax.random.fold_in(streams_of[5], 1), 0, BW - 1).astype(jnp.int32),
    }


def attend_block(query_part, upward_part, pair_rows, allowed):
    row_count = query_part.shape[0]
    key_count = pair_rows.shape[0]
    score_scale = HD ** -0.5
    highest = lax.Precision.HIGHEST
    query_heads = query_part.astype(jnp.float32).reshape(row_count, H, HD)
    upward_heads = upward_part.astype(jnp.float32).reshape(row_count, H, HD)
    key_heads = pair_rows[:, :D].astype(jnp.float32).reshape(key_count, H, HD)
    value_heads = pair_rows[:, D:].astype(jnp.float32).reshape(key_count, H, HD)
    scores = jnp.einsum("qhd,khd->hqk", query_heads, key_heads, precision=highest) * score_scale
    scores = jnp.where(allowed[None], scores, -jnp.inf)
    largest = jnp.max(scores, axis=2, keepdims=True)
    summed = jnp.sum(jnp.exp(scores - largest), axis=2, keepdims=True)
    log_norm = largest + jnp.log(summed)
    weights = jnp.exp(scores - log_norm)
    weights_low = weights.astype(jnp.bfloat16).astype(jnp.float32)
    attended = jnp.einsum("hqk,khd->qhd", weights_low, value_heads, precision=highest).astype(jnp.bfloat16)
    shifted = jnp.einsum("qhd,qhd->hq", upward_heads, attended.astype(jnp.float32), precision=highest)
    weight_grads = jnp.einsum("qhd,khd->hqk", upward_heads, value_heads, precision=highest)
    score_grads = (weights * (weight_grads - shifted[:, :, None])).astype(jnp.bfloat16).astype(jnp.float32)
    query_grad = (jnp.einsum("hqk,khd->qhd", score_grads, key_heads, precision=highest) * score_scale).astype(jnp.bfloat16)
    key_term = jnp.einsum("hqk,qhd->khd", score_grads, query_heads, precision=highest) * score_scale
    value_term = jnp.einsum("hqk,qhd->khd", weights_low, upward_heads, precision=highest)
    pair_terms = jnp.concatenate([key_term.reshape(key_count, D), value_term.reshape(key_count, D)], axis=1)
    return attended.reshape(row_count, D), query_grad.reshape(row_count, D), pair_terms


def first_block(wide_pos, narrow_pos):
    return (wide_pos * N_NARROW + narrow_pos) * BW


def candidate_list(partition, expander_pick):
    wide_pos = partition // N_NARROW
    narrow_pos = partition % N_NARROW
    top_bit = N_WIDE.bit_length() - 1
    own_range = jnp.arange(BW, dtype=jnp.int32)
    left_block = first_block(jnp.maximum(wide_pos - 1, 0), narrow_pos) + BW - 1
    right_block = first_block(jnp.minimum(wide_pos + 1, N_WIDE - 1), narrow_pos)
    lower_blocks = first_block(wide_pos, jnp.maximum(narrow_pos - 1, 0)) + own_range
    upper_blocks = first_block(wide_pos, jnp.minimum(narrow_pos + 1, N_NARROW - 1)) + own_range
    far_blocks = []
    for expander_slot in range(EXP):
        partner = jnp.bitwise_xor(wide_pos, 1 << (top_bit - 1 - expander_slot))
        far_blocks.append(first_block(partner, narrow_pos) + expander_pick[partner * N_NARROW + narrow_pos, expander_slot])
    block_ids = jnp.concatenate([first_block(wide_pos, narrow_pos) + own_range, left_block[None], right_block[None], lower_blocks, upper_blocks, jnp.stack(far_blocks)]).astype(jnp.int32)
    ones_own = jnp.ones((BW,), jnp.int32)
    inside = jnp.concatenate([ones_own, (wide_pos > 0).astype(jnp.int32)[None], (wide_pos < N_WIDE - 1).astype(jnp.int32)[None], ones_own * (narrow_pos > 0).astype(jnp.int32), ones_own * (narrow_pos < N_NARROW - 1).astype(jnp.int32), jnp.ones((EXP,), jnp.int32)])
    return block_ids, inside


def reference(queries, key_rows, value_rows, upstream, pattern, expander_pick):
    partitions = N_WIDE * N_NARROW
    pair_blocks = jnp.concatenate([key_rows, value_rows], axis=1).reshape(partitions * BW, BLK, 2 * D)
    query_parts = queries.reshape(partitions, BW * BLK, D)
    upward_parts = upstream.reshape(partitions, BW * BLK, D)
    pattern_parts = pattern.reshape(partitions, BW, CAND)
    own_marks = (jnp.arange(CAND) < BW)[:, None, None]

    def visit_part(totals, partition):
        block_ids, inside = candidate_list(partition, expander_pick)
        seen = (pattern_parts[partition] * inside[None, :]) > 0
        allowed = jnp.repeat(jnp.repeat(seen, BLK, axis=0), BLK, axis=1)
        pair_rows = pair_blocks[block_ids].reshape(CAND * BLK, 2 * D)
        attended, query_grad, pair_terms = attend_block(query_parts[partition], upward_parts[partition], pair_rows, allowed)
        pair_terms = pair_terms.reshape(CAND, BLK, 2 * D)
        rounded = lax.optimization_barrier(pair_terms.astype(jnp.bfloat16)).astype(jnp.float32)
        terms = jnp.where(own_marks, pair_terms, rounded)
        return totals.at[block_ids].add(terms), (attended, query_grad)

    start = jnp.zeros((partitions * BW, BLK, 2 * D), jnp.float32)
    totals, (attended, query_grad) = lax.scan(visit_part, start, jnp.arange(partitions, dtype=jnp.int32))
    key_grad = totals[:, :, :D].reshape(NODES, D).astype(jnp.bfloat16)
    value_grad = totals[:, :, D:].reshape(NODES, D).astype(jnp.bfloat16)
    return attended.reshape(NODES, D), query_grad.reshape(NODES, D), key_grad, value_grad
```

```python
import jax
import jax.numpy as jnp
from jax import lax
from jax.experimental import pallas as pl
from jax.experimental.pallas import tpu as pltpu
from jax.sharding import PartitionSpec as P

D = 768
HD = 64
BLK = 128
BW = 2
EXP = 3
ROWS = BW * BLK
NEAR = 2 * BW + 2 + BW + 2
PAIRS = D // BLK
GROUP = 6
SCALE = HD ** (-0.5)
LOG2 = SCALE * 1.4426950408889634
HIDDEN = -1e30

VMEM_LIMIT = 40 * 1024 * 1024
NT = (((1,), (1,)), ((), ()))
NN = (((1,), (0,)), ((), ()))
f32 = jnp.float32
bf16 = jnp.bfloat16


def vmem():
    return pl.BlockSpec(memory_space=pltpu.VMEM)


def smem():
    return pl.BlockSpec(memory_space=pltpu.SMEM)


def dot(a, b, dims):
    return lax.dot_general(a, b, dims, preferred_element_type=f32)


def lanes(pair):
    return pl.ds(pl.multiple_of(pair * BLK, BLK), BLK)


def low_lane(shape):
    return lax.broadcasted_iota(jnp.int32, shape, 1) < HD


def low_row(shape):
    return lax.broadcasted_iota(jnp.int32, shape, 0) < HD


def stacked(tile):
    low = low_lane(tile.shape)
    zero = jnp.zeros_like(tile)
    return jnp.concatenate([jnp.where(low, tile, zero), jnp.where(low, zero, tile)], axis=0)


def stacked_t(tile):
    turned = tile.astype(f32).T
    low = low_row(turned.shape)
    zero = jnp.zeros_like(turned)
    return jnp.concatenate(
        [jnp.where(low, turned, zero), jnp.where(low, zero, turned)], axis=1
    ).astype(bf16)


def by_head(stat):
    return jnp.concatenate(
        [jnp.broadcast_to(stat[0:1], (BLK, ROWS)), jnp.broadcast_to(stat[1:2], (BLK, ROWS))], axis=0
    )


def by_feature(stat):
    return jnp.concatenate(
        [jnp.broadcast_to(stat[0:1], (HD, ROWS)), jnp.broadcast_to(stat[1:2], (HD, ROWS))], axis=0
    )


def seen_row(seen0, seen1):
    first = lax.broadcasted_iota(jnp.int32, (1, ROWS), 1) < BLK
    return jnp.where(first, seen0, seen1) > 0


def head_reduce(fn, tile):
    half = tile.shape[0] // 2
    return jnp.concatenate(
        [fn(tile[:half], axis=0, keepdims=True), fn(tile[half:], axis=0, keepdims=True)], axis=0
    )


def scores_t(key_tile, query_tile):
    return dot(stacked(key_tile), query_tile, NT)


def online(keys, values, queries, row, stat_ref, acc_ref, pairs):
    scores = [scores_t(k, q) for k, q in zip(keys, queries)]
    turned = [stacked_t(v) for v in values]
    probs, decays = [], []
    for pair, tile in zip(pairs, scores):
        old = stat_ref[pair, 0:2, :]
        new = jnp.where(row, jnp.maximum(old, head_reduce(jnp.max, tile) * LOG2), old)
        decay = jnp.exp2(old - new)
        weight = jnp.exp2(tile * LOG2 - by_head(jnp.where(row, new, -HIDDEN)))
        stat_ref[pair, 0:2, :] = new
        stat_ref[pair, 2:4, :] = stat_ref[pair, 2:4, :] * decay + head_reduce(jnp.sum, weight)
        probs.append(weight.astype(bf16))
        decays.append(decay)
    for i, pair in enumerate(pairs):
        acc_ref[pair] = acc_ref[pair] * by_feature(decays[i]) + dot(turned[i], probs[i], NN)


def own_head(product):
    return jnp.where(low_lane((BLK, BLK)), product[:BLK], product[BLK:])


def backward(keys, values, queries, upwards, row, stats):
    scores = [scores_t(k, q) for k, q in zip(keys, queries)]
    products = [dot(stacked(v), u, NT) for v, u in zip(values, upwards)]
    weights, grads = [], []
    for tile, product, stat in zip(scores, products, stats):
        weight = jnp.exp2(tile * LOG2 - by_head(jnp.where(row, stat[0:2], -HIDDEN)))
        weights.append(weight.astype(bf16))
        grads.append((weight * (product - by_head(stat[2:4]))).astype(bf16))
    value_terms = [own_head(dot(w, u, NN)).astype(bf16) for w, u in zip(weights, upwards)]
    key_terms = [(own_head(dot(g, q, NN)) * SCALE).astype(bf16) for g, q in zip(grads, queries)]
    query_ts = [dot(stacked_t(k), g, NN) for k, g in zip(keys, grads)]
    return key_terms, value_terms, query_ts


def groups():
    return [range(first, first + GROUP) for first in range(0, PAIRS, GROUP)]


def near_slots(key, value, left, right, lower, upper, far0, far1):
    own = [(key, b * BLK, value, b * BLK) for b in range(BW)]
    rims = [(r, 0, r, BLK) for r in (left, right)]
    sides = [(r, b * BLK, r, ROWS + b * BLK) for r in (lower, upper) for b in range(BW)]
    fars = [(r, 0, r, BLK) for r in (far0, far1)]
    return own + rims + sides + fars


def feature(pair):
    return slice(pair * BLK, (pair + 1) * BLK)


def load_seen(seen, slots, held, place, sems):
    count = jnp.int32(0)
    for j, (k_ref, k_row, v_ref, v_row) in enumerate(slots):
        used = seen[0, j] + seen[1, j] > 0
        at = count

        @pl.when(used)
        def _():
            place[at] = j
            pltpu.make_async_copy(
                k_ref.at[pl.ds(k_row, BLK)], held.at[at, pl.ds(0, BLK)], sems.at[at]
            ).start()
            pltpu.make_async_copy(
                v_ref.at[pl.ds(v_row, BLK)], held.at[at, pl.ds(BLK, BLK)], sems.at[at]
            ).start()

        count = count + used.astype(jnp.int32)
    return count


def await_slot(held, at, sems):
    pltpu.make_async_copy(held.at[at], held.at[at], sems.at[at]).wait()


def forward_kernel(
    seen, query, upward, key, value, left, right, lower, upper, far0, far1, stat, acc, upward_t, held, place, sems
):
    slots = near_slots(key, value, left, right, lower, upper, far0, far1)
    count = load_seen(seen, slots, held, place, sems)
    for pair in range(PAIRS):
        stat[pair, 0:2, :] = jnp.full((2, ROWS), HIDDEN, f32)
        stat[pair, 2:4, :] = jnp.zeros((2, ROWS), f32)
        acc[pair] = jnp.zeros((BLK, ROWS), f32)
        upward_t[pair] = upward[:, feature(pair)].astype(f32).T

    def step(at, carry):
        await_slot(held, at, sems)
        j = place[at]
        row = seen_row(seen[0, j], seen[1, j])
        for pairs in groups():
            online(
                [held[at, 0:BLK, feature(p)] for p in pairs],
                [held[at, BLK : 2 * BLK, feature(p)] for p in pairs],
                [query[:, feature(p)] for p in pairs],
                row,
                stat,
                acc,
                pairs,
            )
        return carry

    lax.fori_loop(0, count, step, 0)


def middle_kernel(
    seen, query, upward, far2, stat_in, acc_in, upward_t, stat, out_t, query_t, term, acc
):
    last = NEAR
    used = seen[0, last] + seen[1, last] > 0
    row = seen_row(seen[0, last], seen[1, last])
    stat[...] = stat_in[...]
    acc[...] = acc_in[...]

    @pl.when(used)
    def _():
        for pairs in groups():
            online(
                [far2[0:BLK, feature(p)] for p in pairs],
                [far2[BLK : 2 * BLK, feature(p)] for p in pairs],
                [query[:, feature(p)] for p in pairs],
                row,
                stat,
                acc,
                pairs,
            )

    for pair in range(PAIRS):
        total = stat[pair, 2:4, :]
        attended = (acc[pair] * by_feature(1.0 / total)).astype(bf16)
        out_t[pair] = attended
        stat[pair, 0:2, :] = stat[pair, 0:2, :] + jnp.log2(total)
        stat[pair, 2:4, :] = head_reduce(jnp.sum, upward_t[pair] * attended.astype(f32))

    @pl.when(used)
    def _():
        for pairs in groups():
            key_terms, value_terms, grads = backward(
                [far2[0:BLK, feature(p)] for p in pairs],
                [far2[BLK : 2 * BLK, feature(p)] for p in pairs],
                [query[:, feature(p)] for p in pairs],
                [upward[:, feature(p)] for p in pairs],
                row,
                [stat[p] for p in pairs],
            )
            for i, pair in enumerate(pairs):
                term[0:BLK, feature(pair)] = key_terms[i]
                term[BLK : 2 * BLK, feature(pair)] = value_terms[i]
                query_t[pair] = grads[i]

    @pl.when(jnp.logical_not(used))
    def _():
        term[...] = jnp.zeros_like(term)
        query_t[...] = jnp.zeros_like(query_t)


def backward_kernel(
    seen,
    query,
    upward,
    key,
    value,
    left,
    right,
    lower,
    upper,
    far0,
    far1,
    stat,
    out_t,
    query_t_in,
    attention,
    query_grad,
    own_key,
    own_value,
    left_term,
    right_term,
    lower_term,
    upper_term,
    far0_term,
    far1_term,
    query_t,
    held,
    terms,
    place,
    sems,
    out_sems,
):
    sources = near_slots(key, value, left, right, lower, upper, far0, far1)
    targets = near_slots(
        own_key, own_value, left_term, right_term, lower_term, upper_term, far0_term, far1_term
    )
    count = load_seen(seen, sources, held, place, sems)
    for pair in range(PAIRS):
        query_t[pair] = query_t_in[pair]
        attention[:, feature(pair)] = out_t[pair].astype(f32).T.astype(bf16)
    terms[len(sources)] = jnp.zeros((2 * BLK, D), bf16)

    def send(j, at):
        k_ref, k_row, v_ref, v_row = targets[j]
        pltpu.make_async_copy(
            terms.at[at, pl.ds(0, BLK)], k_ref.at[pl.ds(k_row, BLK)], out_sems.at[j]
        ).start()
        pltpu.make_async_copy(
            terms.at[at, pl.ds(BLK, BLK)], v_ref.at[pl.ds(v_row, BLK)], out_sems.at[j]
        ).start()

    for j in range(BW, len(targets)):

        @pl.when(seen[0, j] + seen[1, j] == 0)
        def _():
            send(j, len(targets))

    def step(at, carry):
        await_slot(held, at, sems)
        j = place[at]
        row = seen_row(seen[0, j], seen[1, j])
        for pairs in groups():
            key_terms, value_terms, grads = backward(
                [held[at, 0:BLK, feature(p)] for p in pairs],
                [held[at, BLK : 2 * BLK, feature(p)] for p in pairs],
                [query[:, feature(p)] for p in pairs],
                [upward[:, feature(p)] for p in pairs],
                row,
                [stat[p] for p in pairs],
            )
            for i, pair in enumerate(pairs):
                terms[at, 0:BLK, feature(pair)] = key_terms[i]
                terms[at, BLK : 2 * BLK, feature(pair)] = value_terms[i]
                query_t[pair] = query_t[pair] + grads[i]
        for slot in range(len(targets)):

            @pl.when(j == slot)
            def _():
                send(slot, at)

        return carry

    lax.fori_loop(0, count, step, 0)
    for pair in range(PAIRS):
        query_grad[:, feature(pair)] = (query_t[pair] * SCALE).T.astype(bf16)
    for j in range(len(targets)):
        pltpu.make_async_copy(terms.at[0], terms.at[0], out_sems.at[j]).wait()


def sum_kernel(
    pick, own_key, own_value, low_block, high_block, lower, upper, far0, far1, far2, key_grad, value_grad
):
    for half, (own, out) in enumerate(((own_key, key_grad), (own_value, value_grad))):
        for b in range(BW):
            rows = slice(b * BLK, (b + 1) * BLK)
            side = slice(half * ROWS + b * BLK, half * ROWS + (b + 1) * BLK)
            part = slice(half * BLK, (half + 1) * BLK)
            total = own[rows].astype(f32) + lower[side].astype(f32) + upper[side].astype(f32)
            if b == 0:
                total = total + low_block[part].astype(f32)
            if b == BW - 1:
                total = total + high_block[part].astype(f32)
            for slot, far in enumerate((far0, far1, far2)):
                total = total + jnp.where(pick[0, slot] == b, far[part].astype(f32), 0.0)
            out[rows] = total.astype(bf16)


def call(kernel, shapes, specs, args, scratch=(), outs=None, cost=None):
    return pl.pallas_call(
        kernel,
        out_shape=shapes,
        in_specs=specs,
        out_specs=outs if outs is not None else jax.tree.map(lambda _: vmem(), shapes),
        scratch_shapes=list(scratch),
        compiler_params=pltpu.CompilerParams(vmem_limit_bytes=VMEM_LIMIT),
        cost_estimate=cost,
    )(*args)


def shape(dims, dtype):
    return jax.ShapeDtypeStruct(dims, dtype)


def hbm():
    return pl.BlockSpec(memory_space=pl.ANY)


def block_of(key, value, start, out):
    rows = pl.ds(pl.multiple_of(start, BLK), BLK)
    out[0:BLK] = key[rows]
    out[BLK : 2 * BLK] = value[rows]


def pack_far2_kernel(pick, key, value, out):
    block_of(key, value, pick[0, 2] * BLK, out)


def pack_near_kernel(pick, after, key, value, right, left, far0, far1, whole):
    block_of(key, value, 0, right)
    block_of(key, value, ROWS - BLK, left)
    block_of(key, value, pick[0, 0] * BLK, far0)
    block_of(key, value, pick[0, 1] * BLK, far1)
    whole[0:ROWS] = key[...]
    whole[ROWS : 2 * ROWS] = value[...]


def pack_far2(pick, key, value):
    return call(
        pack_far2_kernel, shape((2 * BLK, D), bf16), [smem(), vmem(), vmem()], (pick, key, value)
    )


def pack_near(pick, after, key, value):
    rim = shape((2 * BLK, D), bf16)
    return call(
        pack_near_kernel,
        [rim] * 4 + [shape((2 * ROWS, D), bf16)],
        [smem(), hbm(), vmem(), vmem()],
        (pick, after, key, value),
    )


def run_forward(seen, near):
    return call(
        forward_kernel,
        [shape((PAIRS, 8, ROWS), f32), shape((PAIRS, BLK, ROWS), f32), shape((PAIRS, BLK, ROWS), f32)],
        [smem()] + [vmem()] * 2 + [hbm()] * (len(near) - 2),
        (seen, *near),
        scratch=[
            pltpu.VMEM((NEAR, 2 * BLK, D), bf16),
            pltpu.SMEM((16,), jnp.int32),
            pltpu.SemaphoreType.DMA((NEAR,)),
        ],
    )


def run_middle(seen, queries, upstream, far2, stat, acc, upward_t):
    return call(
        middle_kernel,
        [
            shape((PAIRS, 8, ROWS), f32),
            shape((PAIRS, BLK, ROWS), bf16),
            shape((PAIRS, BLK, ROWS), f32),
            shape((2 * BLK, D), bf16),
        ],
        [smem()] + [vmem()] * 6,
        (seen, queries, upstream, far2, stat, acc, upward_t),
        scratch=[pltpu.VMEM((PAIRS, BLK, ROWS), f32)],
    )


def run_backward(seen, near, stat, out_t, query_t):
    whole = shape((ROWS, D), bf16)
    rim = shape((2 * BLK, D), bf16)
    side = shape((2 * ROWS, D), bf16)
    return call(
        backward_kernel,
        [whole, whole, whole, whole, rim, rim, side, side, rim, rim],
        [smem()] + [vmem()] * 2 + [hbm()] * (len(near) - 2) + [vmem()] * 3,
        (seen, *near, stat, out_t, query_t),
        outs=[vmem()] * 2 + [hbm()] * 8,
        scratch=[
            pltpu.VMEM((PAIRS, BLK, ROWS), f32),
            pltpu.VMEM((NEAR, 2 * BLK, D), bf16),
            pltpu.VMEM((NEAR + 1, 2 * BLK, D), bf16),
            pltpu.SMEM((16,), jnp.int32),
            pltpu.SemaphoreType.DMA((NEAR,)),
            pltpu.SemaphoreType.DMA((NEAR,)),
        ],
    )


def run_sum(pick, args):
    whole = shape((ROWS, D), bf16)
    return call(sum_kernel, [whole, whole], [smem()] + [vmem()] * len(args), (pick, *args))


def partner(value, distance):
    mask = 2**distance
    return lax.ppermute(value, "wide", [(s, s ^ mask) for s in range(lax.axis_size("wide"))])


def shift(value, axis, step):
    count = lax.axis_size(axis)
    pairs = [(s, s + step) for s in range(count) if 0 <= s + step < count]
    return lax.ppermute(value, axis, pairs)


def on_device(queries, key_rows, value_rows, upstream, pattern, expander_pick):
    wide_total = lax.axis_size("wide")
    narrow_total = lax.axis_size("narrow")
    wide_pos = lax.axis_index("wide")
    narrow_pos = lax.axis_index("narrow")
    top_bit = wide_total.bit_length() - 1

    far2_pair = pack_far2(expander_pick, key_rows, value_rows)
    right_pair, left_pair, far0_pair, far1_pair, whole = pack_near(
        expander_pick, far2_pair, key_rows, value_rows
    )
    far2 = partner(far2_pair, top_bit - EXP)
    far0 = partner(far0_pair, top_bit - 1)
    far1 = partner(far1_pair, top_bit - 2)
    right = shift(right_pair, "wide", -1)
    left = shift(left_pair, "wide", 1)
    lower = shift(whole, "narrow", 1)
    upper = shift(whole, "narrow", -1)

    column = jnp.arange(pattern.shape[1])
    away = (
        ((column == 2) & (wide_pos == 0))
        | ((column == 3) & (wide_pos == wide_total - 1))
        | ((column >= 4) & (column < 6) & (narrow_pos == 0))
        | ((column >= 6) & (column < 8) & (narrow_pos == narrow_total - 1))
    )
    seen = jnp.where(away[None, :], 0, pattern)

    near = (queries, upstream, key_rows, value_rows, left, right, lower, upper, far0, far1)
    stat, acc, upward_t = run_forward(seen, near)
    stat, out_t, query_t, far2_term = run_middle(seen, queries, upstream, far2, stat, acc, upward_t)
    far2_back = partner(far2_term, top_bit - EXP)
    (
        attention,
        query_grad,
        own_key,
        own_value,
        left_term,
        right_term,
        lower_term,
        upper_term,
        far0_term,
        far1_term,
    ) = run_backward(seen, near, stat, out_t, query_t)
    key_grad, value_grad = run_sum(
        expander_pick,
        (
            own_key,
            own_value,
            shift(right_term, "wide", 1),
            shift(left_term, "wide", -1),
            shift(upper_term, "narrow", 1),
            shift(lower_term, "narrow", -1),
            partner(far0_term, top_bit - 1),
            partner(far1_term, top_bit - 2),
            far2_back,
        ),
    )
    return (attention, query_grad, key_grad, value_grad)


def solution(mesh):
    placed = P(("wide", "narrow"), None)
    return jax.shard_map(
        on_device,
        mesh=mesh,
        in_specs=(placed,) * 6,
        out_specs=(placed,) * 4,
        check_vma=False,
    )
```

```python
import jax
import jax.numpy as jnp
from jax import lax
from jax.experimental import pallas as pl
from jax.experimental.pallas import tpu as pltpu
from jax.sharding import PartitionSpec as P

D = 768
HD = 64
BLK = 128
BW = 2
EXP = 3
ROWS = BW * BLK
PAIRS = D // BLK
GROUP = 6
SCALE = HD ** (-0.5)
LOG2 = SCALE * 1.4426950408889634
HIDDEN = -1e30

VMEM_LIMIT = 24 * 1024 * 1024
NT = (((1,), (1,)), ((), ()))
NN = (((1,), (0,)), ((), ()))
f32 = jnp.float32
bf16 = jnp.bfloat16


def vmem():
    return pl.BlockSpec(memory_space=pltpu.VMEM)


def smem():
    return pl.BlockSpec(memory_space=pltpu.SMEM)


def dot(a, b, dims):
    return lax.dot_general(a, b, dims, preferred_element_type=f32)


def lanes(pair):
    return pl.ds(pl.multiple_of(pair * BLK, BLK), BLK)


def low_lane(shape):
    return lax.broadcasted_iota(jnp.int32, shape, 1) < HD


def low_row(shape):
    return lax.broadcasted_iota(jnp.int32, shape, 0) < HD


def stacked(tile):
    low = low_lane(tile.shape)
    zero = jnp.zeros_like(tile)
    return jnp.concatenate([jnp.where(low, tile, zero), jnp.where(low, zero, tile)], axis=0)


def stacked_t(tile):
    turned = tile.astype(f32).T
    low = low_row(turned.shape)
    zero = jnp.zeros_like(turned)
    return jnp.concatenate(
        [jnp.where(low, turned, zero), jnp.where(low, zero, turned)], axis=1
    ).astype(bf16)


def by_head(stat):
    return jnp.concatenate(
        [jnp.broadcast_to(stat[0:1], (BLK, ROWS)), jnp.broadcast_to(stat[1:2], (BLK, ROWS))], axis=0
    )


def by_feature(stat):
    return jnp.concatenate(
        [jnp.broadcast_to(stat[0:1], (HD, ROWS)), jnp.broadcast_to(stat[1:2], (HD, ROWS))], axis=0
    )


def seen_row(seen0, seen1):
    first = lax.broadcasted_iota(jnp.int32, (1, ROWS), 1) < BLK
    return jnp.where(first, seen0, seen1) > 0


def head_reduce(fn, tile):
    half = tile.shape[0] // 2
    return jnp.concatenate(
        [fn(tile[:half], axis=0, keepdims=True), fn(tile[half:], axis=0, keepdims=True)], axis=0
    )


def scores_t(key_tile, query_tile):
    return dot(stacked(key_tile), query_tile, NT)


def online(keys, values, queries, row, stat_ref, acc_ref, pairs):
    scores = [scores_t(k, q) for k, q in zip(keys, queries)]
    turned = [stacked_t(v) for v in values]
    probs, decays = [], []
    for pair, tile in zip(pairs, scores):
        old = stat_ref[pair, 0:2, :]
        new = jnp.where(row, jnp.maximum(old, head_reduce(jnp.max, tile) * LOG2), old)
        decay = jnp.exp2(old - new)
        weight = jnp.exp2(tile * LOG2 - by_head(jnp.where(row, new, -HIDDEN)))
        stat_ref[pair, 0:2, :] = new
        stat_ref[pair, 2:4, :] = stat_ref[pair, 2:4, :] * decay + head_reduce(jnp.sum, weight)
        probs.append(weight.astype(bf16))
        decays.append(decay)
    for i, pair in enumerate(pairs):
        acc_ref[pair] = acc_ref[pair] * by_feature(decays[i]) + dot(turned[i], probs[i], NN)


def own_head(product):
    return jnp.where(low_lane((BLK, BLK)), product[:BLK], product[BLK:])


def backward(keys, values, queries, upwards, row, stats):
    scores = [scores_t(k, q) for k, q in zip(keys, queries)]
    products = [dot(stacked(v), u, NT) for v, u in zip(values, upwards)]
    weights, grads = [], []
    for tile, product, stat in zip(scores, products, stats):
        weight = jnp.exp2(tile * LOG2 - by_head(jnp.where(row, stat[0:2], -HIDDEN)))
        weights.append(weight.astype(bf16))
        grads.append((weight * (product - by_head(stat[2:4]))).astype(bf16))
    value_terms = [own_head(dot(w, u, NN)).astype(bf16) for w, u in zip(weights, upwards)]
    key_terms = [(own_head(dot(g, q, NN)) * SCALE).astype(bf16) for g, q in zip(grads, queries)]
    query_ts = [dot(stacked_t(k), g, NN) for k, g in zip(keys, grads)]
    return key_terms, value_terms, query_ts


def groups():
    return [range(first, first + GROUP) for first in range(0, PAIRS, GROUP)]


def own_slots(key, value):
    return [(b, key, b * BLK, value, b * BLK) for b in range(BW)]


def side_slots(chip, cross):
    return [
        (4 + BW * i + b, ref, b * BLK, ref, ROWS + b * BLK)
        for i, ref in enumerate((chip, cross))
        for b in range(BW)
    ]


def pair_slots(columns, *refs):
    return [(j, ref, 0, ref, BLK) for j, ref in zip(columns, refs)]


def rest_slots(left, right, far0, far1):
    return pair_slots((2, 3, 8, 9), left, right, far0, far1)


def rows_at(start):
    return pl.ds(start if isinstance(start, int) else pl.multiple_of(start, BLK), BLK)


def feature(pair):
    return slice(pair * BLK, (pair + 1) * BLK)


def load_seen(seen, slots, held, place):
    count = jnp.int32(0)
    for j, k_ref, k_row, v_ref, v_row in slots:
        used = seen[0, j] + seen[1, j] > 0
        at = count

        @pl.when(used)
        def _():
            place[at] = j
            held[at, 0:BLK] = k_ref[rows_at(k_row)]
            held[at, BLK : 2 * BLK] = v_ref[rows_at(v_row)]

        count = count + used.astype(jnp.int32)
    return count


def forward_over(slots, seen, query, stat, acc, held, place):
    count = load_seen(seen, slots, held, place)

    def step(at, carry):
        j = place[at]
        row = seen_row(seen[0, j], seen[1, j])
        for pairs in groups():
            online(
                [held[at, 0:BLK, feature(p)] for p in pairs],
                [held[at, BLK : 2 * BLK, feature(p)] for p in pairs],
                [query[:, feature(p)] for p in pairs],
                row,
                stat,
                acc,
                pairs,
            )
        return carry

    lax.fori_loop(0, count, step, 0)


def first_kernel(seen, query, upward, key, value, chip, cross, stat, acc, upward_t, held, place):
    for pair in range(PAIRS):
        stat[pair, 0:2, :] = jnp.full((2, ROWS), HIDDEN, f32)
        stat[pair, 2:4, :] = jnp.zeros((2, ROWS), f32)
        acc[pair] = jnp.zeros((BLK, ROWS), f32)
        upward_t[pair] = upward[:, feature(pair)].astype(f32).T
    forward_over(
        own_slots(key, value) + side_slots(chip, cross), seen, query, stat, acc, held, place
    )


def far_kernel(far2, seen, query, stat_in, acc_in, stat, acc, held, place):
    stat[...] = stat_in[...]
    acc[...] = acc_in[...]
    forward_over(pair_slots((10,), far2), seen, query, stat, acc, held, place)


def clear_unseen(slots, seen):
    for j, k_ref, k_row, v_ref, v_row in slots:

        @pl.when(seen[0, j] + seen[1, j] == 0)
        def _():
            k_ref[k_row : k_row + BLK] = jnp.zeros((BLK, D), bf16)
            v_ref[v_row : v_row + BLK] = jnp.zeros((BLK, D), bf16)


def backward_over(sources, seen, query, upward, stat, query_t, held, place, terms, store):
    count = load_seen(seen, sources, held, place)

    def step(at, carry):
        j = place[at]
        row = seen_row(seen[0, j], seen[1, j])
        for pairs in groups():
            key_terms, value_terms, grads = backward(
                [held[at, 0:BLK, feature(p)] for p in pairs],
                [held[at, BLK : 2 * BLK, feature(p)] for p in pairs],
                [query[:, feature(p)] for p in pairs],
                [upward[:, feature(p)] for p in pairs],
                row,
                [stat[p] for p in pairs],
            )
            for i, pair in enumerate(pairs):
                terms[0:BLK, feature(pair)] = key_terms[i]
                terms[BLK : 2 * BLK, feature(pair)] = value_terms[i]
                query_t[pair] = query_t[pair] + grads[i]
        store(j)
        return carry

    lax.fori_loop(0, count, step, 0)


def store_terms(slots, terms, j):
    for slot, k_ref, k_row, v_ref, v_row in slots:

        @pl.when(j == slot)
        def _():
            k_ref[k_row : k_row + BLK] = terms[0:BLK]
            v_ref[v_row : v_row + BLK] = terms[BLK : 2 * BLK]


def middle_kernel(
    far2,
    seen,
    query,
    upward,
    chip,
    cross,
    left,
    right,
    far0,
    far1,
    stat_in,
    acc_in,
    upward_t,
    stat,
    out_t,
    query_t,
    far2_term,
    chip_term,
    cross_term,
    acc,
    terms,
    held,
    place,
):
    stat[...] = stat_in[...]
    acc[...] = acc_in[...]
    forward_over(rest_slots(left, right, far0, far1), seen, query, stat, acc, held, place)

    for pair in range(PAIRS):
        total = stat[pair, 2:4, :]
        attended = (acc[pair] * by_feature(1.0 / total)).astype(bf16)
        out_t[pair] = attended
        stat[pair, 0:2, :] = stat[pair, 0:2, :] + jnp.log2(total)
        stat[pair, 2:4, :] = head_reduce(jnp.sum, upward_t[pair] * attended.astype(f32))

    query_t[...] = jnp.zeros_like(query_t)
    targets = pair_slots((10,), far2_term) + side_slots(chip_term, cross_term)
    clear_unseen(targets, seen)
    backward_over(
        pair_slots((10,), far2) + side_slots(chip, cross),
        seen,
        query,
        upward,
        stat,
        query_t,
        held,
        place,
        terms,
        lambda j: store_terms(targets, terms, j),
    )


def backward_kernel(
    seen,
    query,
    upward,
    key,
    value,
    left,
    right,
    far0,
    far1,
    chip_back,
    cross_back,
    stat,
    out_t,
    query_t_in,
    attention,
    query_grad,
    key_sum,
    value_sum,
    left_term,
    right_term,
    far0_term,
    far1_term,
    query_t,
    terms,
    held,
    place,
):
    query_t[...] = query_t_in[...]
    for pair in range(PAIRS):
        attention[:, feature(pair)] = out_t[pair].astype(f32).T.astype(bf16)
    targets = rest_slots(left_term, right_term, far0_term, far1_term)
    clear_unseen(targets, seen)

    def store(j):
        for b in range(BW):

            @pl.when(j == b)
            def _():
                for half, out in enumerate((key_sum, value_sum)):
                    side = slice(half * ROWS + b * BLK, half * ROWS + (b + 1) * BLK)
                    out[b * BLK : (b + 1) * BLK] = (
                        terms[half * BLK : (half + 1) * BLK].astype(f32)
                        + chip_back[side].astype(f32)
                        + cross_back[side].astype(f32)
                    )

        store_terms(targets, terms, j)

    backward_over(
        own_slots(key, value) + rest_slots(left, right, far0, far1),
        seen,
        query,
        upward,
        stat,
        query_t,
        held,
        place,
        terms,
        store,
    )
    for pair in range(PAIRS):
        query_grad[:, feature(pair)] = (query_t[pair] * SCALE).T.astype(bf16)


def first_sum_kernel(far2, pick, key_near, value_near, key_sum, value_sum):
    for half, (near, out) in enumerate(((key_near, key_sum), (value_near, value_sum))):
        far_part = far2[half * BLK : (half + 1) * BLK].astype(f32)
        for b in range(BW):
            rows = slice(b * BLK, (b + 1) * BLK)
            out[rows] = near[rows] + jnp.where(pick[0, 2] == b, far_part, 0.0)


def second_sum_kernel(pick, key_sum, value_sum, low_block, high_block, far0, far1, key_grad, value_grad):
    for half, (near, out) in enumerate(((key_sum, key_grad), (value_sum, value_grad))):
        part = slice(half * BLK, (half + 1) * BLK)
        for b in range(BW):
            rows = slice(b * BLK, (b + 1) * BLK)
            total = near[rows]
            if b == 0:
                total = total + low_block[part].astype(f32)
            if b == BW - 1:
                total = total + high_block[part].astype(f32)
            for slot, far in enumerate((far0, far1)):
                total = total + jnp.where(pick[0, slot] == b, far[part].astype(f32), 0.0)
            out[rows] = total.astype(bf16)


def call(kernel, shapes, specs, args, scratch=(), outs=None, cost=None):
    return pl.pallas_call(
        kernel,
        out_shape=shapes,
        in_specs=specs,
        out_specs=outs if outs is not None else jax.tree.map(lambda _: vmem(), shapes),
        scratch_shapes=list(scratch),
        compiler_params=pltpu.CompilerParams(vmem_limit_bytes=VMEM_LIMIT),
        cost_estimate=cost,
    )(*args)


def shape(dims, dtype):
    return jax.ShapeDtypeStruct(dims, dtype)


def hbm():
    return pl.BlockSpec(memory_space=pl.ANY)


STATE = [shape((PAIRS, 8, ROWS), f32), shape((PAIRS, BLK, ROWS), f32)]
RIM = shape((2 * BLK, D), bf16)
SIDE = shape((2 * ROWS, D), bf16)


def block_of(key, value, start, out):
    rows = pl.ds(pl.multiple_of(start, BLK), BLK)
    out[0:BLK] = key[rows]
    out[BLK : 2 * BLK] = value[rows]


def pack_first_kernel(pick, key, value, far2, whole):
    block_of(key, value, pick[0, 2] * BLK, far2)
    whole[0:ROWS] = key[...]
    whole[ROWS : 2 * ROWS] = value[...]


def pack_rest_kernel(pick, chip, cross, key, value, right, left, far0, far1):
    block_of(key, value, 0, right)
    block_of(key, value, ROWS - BLK, left)
    block_of(key, value, pick[0, 0] * BLK, far0)
    block_of(key, value, pick[0, 1] * BLK, far1)


def pack_first(pick, key, value):
    return call(pack_first_kernel, [RIM, SIDE], [smem(), vmem(), vmem()], (pick, key, value))


def pack_rest(pick, chip, cross, key, value):
    return call(
        pack_rest_kernel,
        [RIM] * 4,
        [smem(), hbm(), hbm(), vmem(), vmem()],
        (pick, chip, cross, key, value),
    )


def seen_scratch(slots):
    return [pltpu.VMEM((slots, 2 * BLK, D), bf16), pltpu.SMEM((16,), jnp.int32)]


def run_first(plan, queries, upstream, *near):
    return call(
        first_kernel,
        STATE + [shape((PAIRS, BLK, ROWS), f32)],
        [smem()] + [vmem()] * 6,
        (plan, queries, upstream, *near),
        scratch=seen_scratch(6),
    )


def run_far(far2, plan, queries, stat, acc):
    return call(
        far_kernel,
        STATE,
        [vmem(), smem()] + [vmem()] * 3,
        (far2, plan, queries, stat, acc),
        scratch=seen_scratch(1),
    )


def run_middle(far2, plan, *rest):
    return call(
        middle_kernel,
        [STATE[0], shape((PAIRS, BLK, ROWS), bf16), STATE[1], RIM, SIDE, SIDE],
        [vmem(), smem()] + [vmem()] * 11,
        (far2, plan, *rest),
        scratch=[pltpu.VMEM((PAIRS, BLK, ROWS), f32), pltpu.VMEM((2 * BLK, D), bf16)]
        + seen_scratch(5),
    )


def run_backward(plan, *rest):
    whole = shape((ROWS, D), bf16)
    total = shape((ROWS, D), f32)
    return call(
        backward_kernel,
        [whole, whole, total, total] + [RIM] * 4,
        [smem()] + [vmem()] * 13,
        (plan, *rest),
        scratch=[pltpu.VMEM((PAIRS, BLK, ROWS), f32), pltpu.VMEM((2 * BLK, D), bf16)]
        + seen_scratch(6),
    )


def run_first_sum(far2, pick, *rest):
    whole = shape((ROWS, D), f32)
    return call(
        first_sum_kernel, [whole, whole], [vmem(), smem()] + [vmem()] * 2, (far2, pick, *rest)
    )


def run_second_sum(pick, *rest):
    whole = shape((ROWS, D), bf16)
    return call(second_sum_kernel, [whole, whole], [smem()] + [vmem()] * 6, (pick, *rest))


def sides(chip, cross):
    count = lax.axis_size("narrow")
    across = [(i, i + 1) for i in range(1, count - 1, 2)]
    return (
        lax.ppermute(chip, "narrow", [(i, i ^ 1) for i in range(count)]),
        lax.ppermute(cross, "narrow", across + [(b, a) for a, b in across]),
    )


def partner(value, distance):
    mask = 2**distance
    return lax.ppermute(value, "wide", [(s, s ^ mask) for s in range(lax.axis_size("wide"))])


def shift(value, axis, step):
    count = lax.axis_size(axis)
    pairs = [(s, s + step) for s in range(count) if 0 <= s + step < count]
    return lax.ppermute(value, axis, pairs)


def on_device(queries, key_rows, value_rows, upstream, pattern, expander_pick):
    wide_total = lax.axis_size("wide")
    narrow_total = lax.axis_size("narrow")
    wide_pos = lax.axis_index("wide")
    narrow_pos = lax.axis_index("narrow")
    top_bit = wide_total.bit_length() - 1

    even = narrow_pos & 1 == 0
    near_side = jnp.where(even, pattern[:, 6:8], pattern[:, 4:6])
    far_side = jnp.where(even, pattern[:, 4:6], pattern[:, 6:8])
    inner = (narrow_pos > 0) & (narrow_pos < narrow_total - 1)
    plan = jnp.concatenate(
        [
            pattern[:, 0:2],
            jnp.where(wide_pos > 0, pattern[:, 2:3], 0),
            jnp.where(wide_pos < wide_total - 1, pattern[:, 3:4], 0),
            near_side,
            jnp.where(inner, far_side, 0),
            pattern[:, 8:],
        ],
        axis=1,
    )

    far2_pair, whole = pack_first(expander_pick, key_rows, value_rows)
    chip, cross = sides(whole, whole)
    far2 = partner(far2_pair, top_bit - EXP)
    right_pair, left_pair, far0_pair, far1_pair = pack_rest(
        expander_pick, chip, cross, key_rows, value_rows
    )
    rest = (
        shift(left_pair, "wide", 1),
        shift(right_pair, "wide", -1),
        partner(far0_pair, top_bit - 1),
        partner(far1_pair, top_bit - 2),
    )
    stat, acc, upward_t = run_first(plan, queries, upstream, key_rows, value_rows, chip, cross)
    stat, acc = run_far(far2, plan, queries, stat, acc)
    stat, out_t, query_t, far2_term, chip_term, cross_term = run_middle(
        far2, plan, queries, upstream, chip, cross, *rest, stat, acc, upward_t
    )
    far2_back = partner(far2_term, top_bit - EXP)
    attention, query_grad, key_near, value_near, left_term, right_term, far0_term, far1_term = (
        run_backward(
            plan,
            queries,
            upstream,
            key_rows,
            value_rows,
            *rest,
            *sides(chip_term, cross_term),
            stat,
            out_t,
            query_t,
        )
    )
    key_sum, value_sum = run_first_sum(far2_back, expander_pick, key_near, value_near)
    key_grad, value_grad = run_second_sum(
        expander_pick,
        key_sum,
        value_sum,
        shift(right_term, "wide", 1),
        shift(left_term, "wide", -1),
        partner(far0_term, top_bit - 1),
        partner(far1_term, top_bit - 2),
    )
    return (attention, query_grad, key_grad, value_grad)


def solution(mesh):
    placed = P(("wide", "narrow"), None)
    return jax.shard_map(
        on_device,
        mesh=mesh,
        in_specs=(placed,) * 6,
        out_specs=(placed,) * 4,
        check_vma=False,
    )
```

```python
import jax
import jax.numpy as jnp
from jax import lax
from jax.experimental import pallas as pl
from jax.experimental.pallas import tpu as pltpu
from jax.sharding import PartitionSpec as P

D = 768
HD = 64
BLK = 128
BW = 2
EXP = 3
ROWS = BW * BLK
PAIRS = D // BLK
GROUP = 6
SCALE = HD ** (-0.5)
LOG2 = SCALE * 1.4426950408889634
HIDDEN = -1e30

VMEM_LIMIT = 24 * 1024 * 1024
NT = (((1,), (1,)), ((), ()))
NN = (((1,), (0,)), ((), ()))
f32 = jnp.float32
bf16 = jnp.bfloat16


def vmem():
    return pl.BlockSpec(memory_space=pltpu.VMEM)


def smem():
    return pl.BlockSpec(memory_space=pltpu.SMEM)


def dot(a, b, dims):
    return lax.dot_general(a, b, dims, preferred_element_type=f32)


def lanes(pair):
    return pl.ds(pl.multiple_of(pair * BLK, BLK), BLK)


def low_lane(shape):
    return lax.broadcasted_iota(jnp.int32, shape, 1) < HD


def low_row(shape):
    return lax.broadcasted_iota(jnp.int32, shape, 0) < HD


def stacked(tile):
    low = low_lane(tile.shape)
    zero = jnp.zeros_like(tile)
    return jnp.concatenate([jnp.where(low, tile, zero), jnp.where(low, zero, tile)], axis=0)


def stacked_t(tile):
    turned = tile.astype(f32).T
    low = low_row(turned.shape)
    zero = jnp.zeros_like(turned)
    return jnp.concatenate(
        [jnp.where(low, turned, zero), jnp.where(low, zero, turned)], axis=1
    ).astype(bf16)


def by_head(stat):
    return jnp.concatenate(
        [jnp.broadcast_to(stat[0:1], (BLK, ROWS)), jnp.broadcast_to(stat[1:2], (BLK, ROWS))], axis=0
    )


def by_feature(stat):
    return jnp.concatenate(
        [jnp.broadcast_to(stat[0:1], (HD, ROWS)), jnp.broadcast_to(stat[1:2], (HD, ROWS))], axis=0
    )


def seen_row(seen0, seen1):
    first = lax.broadcasted_iota(jnp.int32, (1, ROWS), 1) < BLK
    return jnp.where(first, seen0, seen1) > 0


def head_reduce(fn, tile):
    half = tile.shape[0] // 2
    return jnp.concatenate(
        [fn(tile[:half], axis=0, keepdims=True), fn(tile[half:], axis=0, keepdims=True)], axis=0
    )


def scores_t(key_tile, query_tile):
    return dot(stacked(key_tile), query_tile, NT)


def online(keys, values, queries, row, stat_ref, acc_ref, pairs):
    scores = [scores_t(k, q) for k, q in zip(keys, queries)]
    turned = [stacked_t(v) for v in values]
    probs, decays = [], []
    for pair, tile in zip(pairs, scores):
        old = stat_ref[pair, 0:2, :]
        new = jnp.where(row, jnp.maximum(old, head_reduce(jnp.max, tile) * LOG2), old)
        decay = jnp.exp2(old - new)
        weight = jnp.exp2(tile * LOG2 - by_head(jnp.where(row, new, -HIDDEN)))
        stat_ref[pair, 0:2, :] = new
        stat_ref[pair, 2:4, :] = stat_ref[pair, 2:4, :] * decay + head_reduce(jnp.sum, weight)
        probs.append(weight.astype(bf16))
        decays.append(decay)
    for i, pair in enumerate(pairs):
        acc_ref[pair] = acc_ref[pair] * by_feature(decays[i]) + dot(turned[i], probs[i], NN)


def own_head(product):
    return jnp.where(low_lane((BLK, BLK)), product[:BLK], product[BLK:])


def backward(keys, values, queries, upwards, row, stats):
    scores = [scores_t(k, q) for k, q in zip(keys, queries)]
    products = [dot(stacked(v), u, NT) for v, u in zip(values, upwards)]
    weights, grads = [], []
    for tile, product, stat in zip(scores, products, stats):
        weight = jnp.exp2(tile * LOG2 - by_head(jnp.where(row, stat[0:2], -HIDDEN)))
        weights.append(weight.astype(bf16))
        grads.append((weight * (product - by_head(stat[2:4]))).astype(bf16))
    value_terms = [own_head(dot(w, u, NN)).astype(bf16) for w, u in zip(weights, upwards)]
    key_terms = [(own_head(dot(g, q, NN)) * SCALE).astype(bf16) for g, q in zip(grads, queries)]
    query_ts = [dot(stacked_t(k), g, NN) for k, g in zip(keys, grads)]
    return key_terms, value_terms, query_ts


def groups():
    return [range(first, first + GROUP) for first in range(0, PAIRS, GROUP)]


def own_slots(whole):
    return [(b, whole, b * BLK, whole, ROWS + b * BLK) for b in range(BW)]


def near_slots(chip, cross, left, right):
    sides = [
        (4 + BW * i + b, ref, b * BLK, ref, ROWS + b * BLK)
        for i, ref in enumerate((chip, cross))
        for b in range(BW)
    ]
    return pair_slots((2, 3), left, right) + sides


def pair_slots(columns, *refs):
    return [(j, ref, 0, ref, BLK) for j, ref in zip(columns, refs)]


def rows_at(start):
    return pl.ds(start if isinstance(start, int) else pl.multiple_of(start, BLK), BLK)


def feature(pair):
    return slice(pair * BLK, (pair + 1) * BLK)


def load_seen(seen, slots, held, place):
    count = jnp.int32(0)
    for j, k_ref, k_row, v_ref, v_row in slots:
        used = seen[0, j] + seen[1, j] > 0
        at = count

        @pl.when(used)
        def _():
            place[at] = j
            held[at, 0:BLK] = k_ref[rows_at(k_row)]
            held[at, BLK : 2 * BLK] = v_ref[rows_at(v_row)]

        count = count + used.astype(jnp.int32)
    return count


def forward_over(slots, seen, query, stat, acc, held, place):
    count = load_seen(seen, slots, held, place)

    def step(at, carry):
        j = place[at]
        row = seen_row(seen[0, j], seen[1, j])
        for pairs in groups():
            online(
                [held[at, 0:BLK, feature(p)] for p in pairs],
                [held[at, BLK : 2 * BLK, feature(p)] for p in pairs],
                [query[:, feature(p)] for p in pairs],
                row,
                stat,
                acc,
                pairs,
            )
        return carry

    lax.fori_loop(0, count, step, 0)


def first_kernel(
    seen, query, upward, whole, chip, cross, left, right, stat, acc, upward_t, held, place
):
    for pair in range(PAIRS):
        stat[pair, 0:2, :] = jnp.full((2, ROWS), HIDDEN, f32)
        stat[pair, 2:4, :] = jnp.zeros((2, ROWS), f32)
        acc[pair] = jnp.zeros((BLK, ROWS), f32)
        upward_t[pair] = upward[:, feature(pair)].astype(f32).T
    forward_over(
        own_slots(whole) + near_slots(chip, cross, left, right), seen, query, stat, acc, held, place
    )


def far_kernel(far2, seen, query, stat_in, acc_in, stat, acc, held, place):
    stat[...] = stat_in[...]
    acc[...] = acc_in[...]
    forward_over(pair_slots((10,), far2), seen, query, stat, acc, held, place)


def clear_unseen(slots, seen):
    for j, k_ref, k_row, v_ref, v_row in slots:

        @pl.when(seen[0, j] + seen[1, j] == 0)
        def _():
            k_ref[k_row : k_row + BLK] = jnp.zeros((BLK, D), bf16)
            v_ref[v_row : v_row + BLK] = jnp.zeros((BLK, D), bf16)


def backward_over(sources, seen, query, upward, stat, query_t, held, place, terms, store):
    count = load_seen(seen, sources, held, place)

    def step(at, carry):
        j = place[at]
        row = seen_row(seen[0, j], seen[1, j])
        for pairs in groups():
            key_terms, value_terms, grads = backward(
                [held[at, 0:BLK, feature(p)] for p in pairs],
                [held[at, BLK : 2 * BLK, feature(p)] for p in pairs],
                [query[:, feature(p)] for p in pairs],
                [upward[:, feature(p)] for p in pairs],
                row,
                [stat[p] for p in pairs],
            )
            for i, pair in enumerate(pairs):
                terms[0:BLK, feature(pair)] = key_terms[i]
                terms[BLK : 2 * BLK, feature(pair)] = value_terms[i]
                query_t[pair] = query_t[pair] + grads[i]
        store(j)
        return carry

    lax.fori_loop(0, count, step, 0)


def store_terms(slots, terms, j):
    for slot, k_ref, k_row, v_ref, v_row in slots:

        @pl.when(j == slot)
        def _():
            k_ref[k_row : k_row + BLK] = terms[0:BLK]
            v_ref[v_row : v_row + BLK] = terms[BLK : 2 * BLK]


def middle_kernel(
    far2,
    seen,
    query,
    upward,
    chip,
    cross,
    left,
    right,
    far0,
    far1,
    stat_in,
    acc_in,
    upward_t,
    stat,
    out_t,
    query_t,
    far2_term,
    chip_term,
    cross_term,
    left_term,
    right_term,
    acc,
    terms,
    held,
    place,
):
    stat[...] = stat_in[...]
    acc[...] = acc_in[...]
    forward_over(pair_slots((8, 9), far0, far1), seen, query, stat, acc, held, place)

    for pair in range(PAIRS):
        total = stat[pair, 2:4, :]
        attended = (acc[pair] * by_feature(1.0 / total)).astype(bf16)
        out_t[pair] = attended
        stat[pair, 0:2, :] = stat[pair, 0:2, :] + jnp.log2(total)
        stat[pair, 2:4, :] = head_reduce(jnp.sum, upward_t[pair] * attended.astype(f32))

    query_t[...] = jnp.zeros_like(query_t)
    targets = pair_slots((10,), far2_term) + near_slots(
        chip_term, cross_term, left_term, right_term
    )
    clear_unseen(targets, seen)
    backward_over(
        pair_slots((10,), far2) + near_slots(chip, cross, left, right),
        seen,
        query,
        upward,
        stat,
        query_t,
        held,
        place,
        terms,
        lambda j: store_terms(targets, terms, j),
    )


def backward_kernel(
    seen,
    query,
    upward,
    whole,
    far0,
    far1,
    chip_back,
    cross_back,
    low_block,
    high_block,
    stat,
    out_t,
    query_t_in,
    attention,
    query_grad,
    key_sum,
    value_sum,
    far0_term,
    far1_term,
    query_t,
    terms,
    held,
    place,
):
    query_t[...] = query_t_in[...]
    for pair in range(PAIRS):
        attention[:, feature(pair)] = out_t[pair].astype(f32).T.astype(bf16)
    targets = pair_slots((8, 9), far0_term, far1_term)
    clear_unseen(targets, seen)

    def store(j):
        for b in range(BW):

            @pl.when(j == b)
            def _():
                for half, out in enumerate((key_sum, value_sum)):
                    side = slice(half * ROWS + b * BLK, half * ROWS + (b + 1) * BLK)
                    part = slice(half * BLK, (half + 1) * BLK)
                    total = terms[part].astype(f32)
                    total = total + chip_back[side].astype(f32) + cross_back[side].astype(f32)
                    if b == 0:
                        total = total + low_block[part].astype(f32)
                    if b == BW - 1:
                        total = total + high_block[part].astype(f32)
                    out[b * BLK : (b + 1) * BLK] = total

        store_terms(targets, terms, j)

    backward_over(
        own_slots(whole) + pair_slots((8, 9), far0, far1),
        seen,
        query,
        upward,
        stat,
        query_t,
        held,
        place,
        terms,
        store,
    )
    for pair in range(PAIRS):
        query_grad[:, feature(pair)] = (query_t[pair] * SCALE).T.astype(bf16)


def first_sum_kernel(far2, pick, key_near, value_near, key_sum, value_sum):
    for half, (near, out) in enumerate(((key_near, key_sum), (value_near, value_sum))):
        far_part = far2[half * BLK : (half + 1) * BLK].astype(f32)
        for b in range(BW):
            rows = slice(b * BLK, (b + 1) * BLK)
            out[rows] = near[rows] + jnp.where(pick[0, 2] == b, far_part, 0.0)


def second_sum_kernel(pick, key_sum, value_sum, far0, far1, key_grad, value_grad):
    for half, (near, out) in enumerate(((key_sum, key_grad), (value_sum, value_grad))):
        part = slice(half * BLK, (half + 1) * BLK)
        for b in range(BW):
            rows = slice(b * BLK, (b + 1) * BLK)
            total = near[rows]
            for slot, far in enumerate((far0, far1)):
                total = total + jnp.where(pick[0, slot] == b, far[part].astype(f32), 0.0)
            out[rows] = total.astype(bf16)


def call(kernel, shapes, specs, args, scratch=(), outs=None, cost=None):
    return pl.pallas_call(
        kernel,
        out_shape=shapes,
        in_specs=specs,
        out_specs=outs if outs is not None else jax.tree.map(lambda _: vmem(), shapes),
        scratch_shapes=list(scratch),
        compiler_params=pltpu.CompilerParams(vmem_limit_bytes=VMEM_LIMIT),
        cost_estimate=cost,
    )(*args)


def shape(dims, dtype):
    return jax.ShapeDtypeStruct(dims, dtype)


def hbm():
    return pl.BlockSpec(memory_space=pl.ANY)


STATE = [shape((PAIRS, 8, ROWS), f32), shape((PAIRS, BLK, ROWS), f32)]
RIM = shape((2 * BLK, D), bf16)
SIDE = shape((2 * ROWS, D), bf16)


def block_of(whole, start, out):
    for half in range(2):
        rows = pl.ds(pl.multiple_of(half * ROWS + start, BLK), BLK)
        out[half * BLK : (half + 1) * BLK] = whole[rows]


def pack_first_kernel(pick, key, value, whole, right, left, far2, sems):
    copies = [
        pltpu.make_async_copy(ref, whole.at[pl.ds(half * ROWS, ROWS)], sems.at[half])
        for half, ref in enumerate((key, value))
    ]
    for one in copies:
        one.start()
    for one in copies:
        one.wait()
    block_of(whole, 0, right)
    block_of(whole, ROWS - BLK, left)
    block_of(whole, pick[0, 2] * BLK, far2)


def pack_rest_kernel(pick, chip, cross, left, right, whole, far0, far1):
    block_of(whole, pick[0, 0] * BLK, far0)
    block_of(whole, pick[0, 1] * BLK, far1)


def pack_first(pick, key, value):
    return call(
        pack_first_kernel,
        [SIDE, RIM, RIM, RIM],
        [smem(), hbm(), hbm()],
        (pick, key, value),
        scratch=[pltpu.SemaphoreType.DMA((2,))],
    )


def pack_rest(pick, *rest):
    return call(
        pack_rest_kernel, [RIM] * 2, [smem()] + [hbm()] * 4 + [vmem()], (pick, *rest)
    )


def seen_scratch(slots):
    return [pltpu.VMEM((slots, 2 * BLK, D), bf16), pltpu.SMEM((16,), jnp.int32)]


def run_first(plan, *rest):
    return call(
        first_kernel,
        STATE + [shape((PAIRS, BLK, ROWS), f32)],
        [smem()] + [vmem()] * 7,
        (plan, *rest),
        scratch=seen_scratch(8),
    )


def run_far(far2, plan, queries, stat, acc):
    return call(
        far_kernel,
        STATE,
        [vmem(), smem()] + [vmem()] * 3,
        (far2, plan, queries, stat, acc),
        scratch=seen_scratch(1),
    )


def run_middle(far2, plan, *rest):
    return call(
        middle_kernel,
        [STATE[0], shape((PAIRS, BLK, ROWS), bf16), STATE[1], RIM, SIDE, SIDE, RIM, RIM],
        [vmem(), smem()] + [vmem()] * 11,
        (far2, plan, *rest),
        scratch=[pltpu.VMEM((PAIRS, BLK, ROWS), f32), pltpu.VMEM((2 * BLK, D), bf16)]
        + seen_scratch(7),
    )


def run_backward(plan, *rest):
    whole = shape((ROWS, D), bf16)
    total = shape((ROWS, D), f32)
    return call(
        backward_kernel,
        [whole, whole, total, total, RIM, RIM],
        [smem()] + [vmem()] * 12,
        (plan, *rest),
        scratch=[pltpu.VMEM((PAIRS, BLK, ROWS), f32), pltpu.VMEM((2 * BLK, D), bf16)]
        + seen_scratch(4),
    )


def run_first_sum(far2, pick, *rest):
    whole = shape((ROWS, D), f32)
    return call(
        first_sum_kernel, [whole, whole], [vmem(), smem()] + [vmem()] * 2, (far2, pick, *rest)
    )


def run_second_sum(pick, *rest):
    whole = shape((ROWS, D), bf16)
    return call(second_sum_kernel, [whole, whole], [smem()] + [vmem()] * 4, (pick, *rest))


def sides(chip, cross):
    count = lax.axis_size("narrow")
    across = [(i, i + 1) for i in range(1, count - 1, 2)]
    return (
        lax.ppermute(chip, "narrow", [(i, i ^ 1) for i in range(count)]),
        lax.ppermute(cross, "narrow", across + [(b, a) for a, b in across]),
    )


def partner(value, distance):
    mask = 2**distance
    return lax.ppermute(value, "wide", [(s, s ^ mask) for s in range(lax.axis_size("wide"))])


def shift(value, axis, step):
    count = lax.axis_size(axis)
    pairs = [(s, s + step) for s in range(count) if 0 <= s + step < count]
    return lax.ppermute(value, axis, pairs)


def on_device(queries, key_rows, value_rows, upstream, pattern, expander_pick):
    wide_total = lax.axis_size("wide")
    narrow_total = lax.axis_size("narrow")
    wide_pos = lax.axis_index("wide")
    narrow_pos = lax.axis_index("narrow")
    top_bit = wide_total.bit_length() - 1

    even = narrow_pos & 1 == 0
    near_side = jnp.where(even, pattern[:, 6:8], pattern[:, 4:6])
    far_side = jnp.where(even, pattern[:, 4:6], pattern[:, 6:8])
    inner = (narrow_pos > 0) & (narrow_pos < narrow_total - 1)
    plan = jnp.concatenate(
        [
            pattern[:, 0:2],
            jnp.where(wide_pos > 0, pattern[:, 2:3], 0),
            jnp.where(wide_pos < wide_total - 1, pattern[:, 3:4], 0),
            near_side,
            jnp.where(inner, far_side, 0),
            pattern[:, 8:],
        ],
        axis=1,
    )

    whole, right_pair, left_pair, far2_pair = pack_first(expander_pick, key_rows, value_rows)
    near = (*sides(whole, whole), shift(left_pair, "wide", 1), shift(right_pair, "wide", -1))
    far2 = partner(far2_pair, top_bit - EXP)
    far0_pair, far1_pair = pack_rest(expander_pick, *near, whole)
    far = (partner(far0_pair, top_bit - 1), partner(far1_pair, top_bit - 2))
    stat, acc, upward_t = run_first(plan, queries, upstream, whole, *near)
    stat, acc = run_far(far2, plan, queries, stat, acc)
    stat, out_t, query_t, far2_term, chip_term, cross_term, left_term, right_term = run_middle(
        far2, plan, queries, upstream, *near, *far, stat, acc, upward_t
    )
    far2_back = partner(far2_term, top_bit - EXP)
    attention, query_grad, key_near, value_near, far0_term, far1_term = run_backward(
        plan,
        queries,
        upstream,
        whole,
        *far,
        *sides(chip_term, cross_term),
        shift(right_term, "wide", 1),
        shift(left_term, "wide", -1),
        stat,
        out_t,
        query_t,
    )
    key_sum, value_sum = run_first_sum(far2_back, expander_pick, key_near, value_near)
    key_grad, value_grad = run_second_sum(
        expander_pick,
        key_sum,
        value_sum,
        partner(far0_term, top_bit - 1),
        partner(far1_term, top_bit - 2),
    )
    return (attention, query_grad, key_grad, value_grad)


def solution(mesh):
    placed = P(("wide", "narrow"), None)
    return jax.shard_map(
        on_device,
        mesh=mesh,
        in_specs=(placed,) * 6,
        out_specs=(placed,) * 4,
        check_vma=False,
    )
```

```python
import jax
import jax.numpy as jnp
from jax import lax
from jax.experimental import pallas as pl
from jax.experimental.pallas import tpu as pltpu
from jax.sharding import PartitionSpec as P

D = 768
HD = 64
BLK = 128
BW = 2
EXP = 3
ROWS = BW * BLK
PAIRS = D // BLK
GROUP = 6
SCALE = HD ** (-0.5)
LOG2 = SCALE * 1.4426950408889634
HIDDEN = -1e30

VMEM_LIMIT = 24 * 1024 * 1024
NT = (((1,), (1,)), ((), ()))
NN = (((1,), (0,)), ((), ()))
f32 = jnp.float32
bf16 = jnp.bfloat16


def vmem():
    return pl.BlockSpec(memory_space=pltpu.VMEM)


def smem():
    return pl.BlockSpec(memory_space=pltpu.SMEM)


def dot(a, b, dims):
    return lax.dot_general(a, b, dims, preferred_element_type=f32)


def lanes(pair):
    return pl.ds(pl.multiple_of(pair * BLK, BLK), BLK)


def low_lane(shape):
    return lax.broadcasted_iota(jnp.int32, shape, 1) < HD


def low_row(shape):
    return lax.broadcasted_iota(jnp.int32, shape, 0) < HD


def stacked(tile):
    low = low_lane(tile.shape)
    zero = jnp.zeros_like(tile)
    return jnp.concatenate([jnp.where(low, tile, zero), jnp.where(low, zero, tile)], axis=0)


def stacked_t(tile):
    turned = tile.astype(f32).T
    low = low_row(turned.shape)
    zero = jnp.zeros_like(turned)
    return jnp.concatenate(
        [jnp.where(low, turned, zero), jnp.where(low, zero, turned)], axis=1
    ).astype(bf16)


def by_head(stat):
    return jnp.concatenate(
        [jnp.broadcast_to(stat[0:1], (BLK, ROWS)), jnp.broadcast_to(stat[1:2], (BLK, ROWS))], axis=0
    )


def by_feature(stat):
    return jnp.concatenate(
        [jnp.broadcast_to(stat[0:1], (HD, ROWS)), jnp.broadcast_to(stat[1:2], (HD, ROWS))], axis=0
    )


def seen_row(seen0, seen1):
    first = lax.broadcasted_iota(jnp.int32, (1, ROWS), 1) < BLK
    return jnp.where(first, seen0, seen1) > 0


def head_reduce(fn, tile):
    half = tile.shape[0] // 2
    return jnp.concatenate(
        [fn(tile[:half], axis=0, keepdims=True), fn(tile[half:], axis=0, keepdims=True)], axis=0
    )


def scores_t(key_tile, query_tile):
    return dot(stacked(key_tile), query_tile, NT)


def online(keys, values, queries, row, stat_ref, acc_ref, pairs):
    scores = [scores_t(k, q) for k, q in zip(keys, queries)]
    turned = [stacked_t(v) for v in values]
    probs, decays = [], []
    for pair, tile in zip(pairs, scores):
        old = stat_ref[pair, 0:2, :]
        new = jnp.where(row, jnp.maximum(old, head_reduce(jnp.max, tile) * LOG2), old)
        decay = jnp.exp2(old - new)
        weight = jnp.exp2(tile * LOG2 - by_head(jnp.where(row, new, -HIDDEN)))
        stat_ref[pair, 0:2, :] = new
        stat_ref[pair, 2:4, :] = stat_ref[pair, 2:4, :] * decay + head_reduce(jnp.sum, weight)
        probs.append(weight.astype(bf16))
        decays.append(decay)
    for i, pair in enumerate(pairs):
        acc_ref[pair] = acc_ref[pair] * by_feature(decays[i]) + dot(turned[i], probs[i], NN)


def own_head(product):
    return jnp.where(low_lane((BLK, BLK)), product[:BLK], product[BLK:])


def backward(keys, values, queries, upwards, row, stats):
    scores = [scores_t(k, q) for k, q in zip(keys, queries)]
    products = [dot(stacked(v), u, NT) for v, u in zip(values, upwards)]
    weights, grads = [], []
    for tile, product, stat in zip(scores, products, stats):
        weight = jnp.exp2(tile * LOG2 - by_head(jnp.where(row, stat[0:2], -HIDDEN)))
        weights.append(weight.astype(bf16))
        grads.append((weight * (product - by_head(stat[2:4]))).astype(bf16))
    value_terms = [own_head(dot(w, u, NN)).astype(bf16) for w, u in zip(weights, upwards)]
    key_terms = [(own_head(dot(g, q, NN)) * SCALE).astype(bf16) for g, q in zip(grads, queries)]
    query_ts = [dot(stacked_t(k), g, NN) for k, g in zip(keys, grads)]
    return key_terms, value_terms, query_ts


def groups():
    return [range(first, first + GROUP) for first in range(0, PAIRS, GROUP)]


def own_slots(key, value):
    return [(b, key, b * BLK, value, b * BLK) for b in range(BW)]


def side_slots(chip, cross):
    return [
        (4 + BW * i + b, ref, b * BLK, ref, ROWS + b * BLK)
        for i, ref in enumerate((chip, cross))
        for b in range(BW)
    ]


def pair_slots(columns, *refs):
    return [(j, ref, 0, ref, BLK) for j, ref in zip(columns, refs)]


def rest_slots(left, right, far0, far1):
    return pair_slots((2, 3, 8, 9), left, right, far0, far1)


def rows_at(start):
    return pl.ds(start if isinstance(start, int) else pl.multiple_of(start, BLK), BLK)


def feature(pair):
    return slice(pair * BLK, (pair + 1) * BLK)


def load_seen(seen, slots, held, place):
    count = jnp.int32(0)
    for j, k_ref, k_row, v_ref, v_row in slots:
        used = seen[0, j] + seen[1, j] > 0
        at = count

        @pl.when(used)
        def _():
            place[at] = j
            held[at, 0:BLK] = k_ref[rows_at(k_row)]
            held[at, BLK : 2 * BLK] = v_ref[rows_at(v_row)]

        count = count + used.astype(jnp.int32)
    return count


def forward_over(slots, seen, query, stat, acc, held, place):
    count = load_seen(seen, slots, held, place)

    def step(at, carry):
        j = place[at]
        row = seen_row(seen[0, j], seen[1, j])
        for pairs in groups():
            online(
                [held[at, 0:BLK, feature(p)] for p in pairs],
                [held[at, BLK : 2 * BLK, feature(p)] for p in pairs],
                [query[:, feature(p)] for p in pairs],
                row,
                stat,
                acc,
                pairs,
            )
        return carry

    lax.fori_loop(0, count, step, 0)


def first_kernel(seen, query, upward, key, value, chip, cross, stat, acc, upward_t, held, place):
    for pair in range(PAIRS):
        stat[pair, 0:2, :] = jnp.full((2, ROWS), HIDDEN, f32)
        stat[pair, 2:4, :] = jnp.zeros((2, ROWS), f32)
        acc[pair] = jnp.zeros((BLK, ROWS), f32)
        upward_t[pair] = upward[:, feature(pair)].astype(f32).T
    forward_over(
        own_slots(key, value) + side_slots(chip, cross), seen, query, stat, acc, held, place
    )


def far_kernel(far2, seen, query, stat_in, acc_in, stat, acc, held, place):
    stat[...] = stat_in[...]
    acc[...] = acc_in[...]
    forward_over(pair_slots((10,), far2), seen, query, stat, acc, held, place)


def clear_unseen(slots, seen):
    for j, k_ref, k_row, v_ref, v_row in slots:

        @pl.when(seen[0, j] + seen[1, j] == 0)
        def _():
            k_ref[k_row : k_row + BLK] = jnp.zeros((BLK, D), bf16)
            v_ref[v_row : v_row + BLK] = jnp.zeros((BLK, D), bf16)


def backward_over(sources, seen, query, upward, stat, query_t, held, place, terms, store):
    count = load_seen(seen, sources, held, place)

    def step(at, carry):
        j = place[at]
        row = seen_row(seen[0, j], seen[1, j])
        for pairs in groups():
            key_terms, value_terms, grads = backward(
                [held[at, 0:BLK, feature(p)] for p in pairs],
                [held[at, BLK : 2 * BLK, feature(p)] for p in pairs],
                [query[:, feature(p)] for p in pairs],
                [upward[:, feature(p)] for p in pairs],
                row,
                [stat[p] for p in pairs],
            )
            for i, pair in enumerate(pairs):
                terms[0:BLK, feature(pair)] = key_terms[i]
                terms[BLK : 2 * BLK, feature(pair)] = value_terms[i]
                query_t[pair] = query_t[pair] + grads[i]
        store(j)
        return carry

    lax.fori_loop(0, count, step, 0)


def store_terms(slots, terms, j):
    for slot, k_ref, k_row, v_ref, v_row in slots:

        @pl.when(j == slot)
        def _():
            k_ref[k_row : k_row + BLK] = terms[0:BLK]
            v_ref[v_row : v_row + BLK] = terms[BLK : 2 * BLK]


def middle_kernel(
    far2,
    seen,
    query,
    upward,
    chip,
    cross,
    left,
    right,
    far0,
    far1,
    stat_in,
    acc_in,
    upward_t,
    stat,
    out_t,
    query_t,
    far2_term,
    chip_term,
    cross_term,
    acc,
    terms,
    held,
    place,
):
    stat[...] = stat_in[...]
    acc[...] = acc_in[...]
    forward_over(rest_slots(left, right, far0, far1), seen, query, stat, acc, held, place)

    for pair in range(PAIRS):
        total = stat[pair, 2:4, :]
        attended = (acc[pair] * by_feature(1.0 / total)).astype(bf16)
        out_t[pair] = attended
        stat[pair, 0:2, :] = stat[pair, 0:2, :] + jnp.log2(total)
        stat[pair, 2:4, :] = head_reduce(jnp.sum, upward_t[pair] * attended.astype(f32))

    query_t[...] = jnp.zeros_like(query_t)
    targets = pair_slots((10,), far2_term) + side_slots(chip_term, cross_term)
    clear_unseen(targets, seen)
    backward_over(
        pair_slots((10,), far2) + side_slots(chip, cross),
        seen,
        query,
        upward,
        stat,
        query_t,
        held,
        place,
        terms,
        lambda j: store_terms(targets, terms, j),
    )


def rest_kernel(
    seen,
    query,
    upward,
    left,
    right,
    far0,
    far1,
    chip_back,
    cross_back,
    stat,
    query_t_in,
    left_term,
    right_term,
    far0_term,
    far1_term,
    query_t,
    terms,
    held,
    place,
):
    query_t[...] = query_t_in[...]
    targets = rest_slots(left_term, right_term, far0_term, far1_term)
    clear_unseen(targets, seen)
    backward_over(
        rest_slots(left, right, far0, far1),
        seen,
        query,
        upward,
        stat,
        query_t,
        held,
        place,
        terms,
        lambda j: store_terms(targets, terms, j),
    )


def own_kernel(
    seen,
    query,
    upward,
    key,
    value,
    chip_back,
    cross_back,
    stat,
    out_t,
    query_t_in,
    attention,
    query_grad,
    key_sum,
    value_sum,
    query_t,
    terms,
    held,
    place,
):
    query_t[...] = query_t_in[...]
    for pair in range(PAIRS):
        attention[:, feature(pair)] = out_t[pair].astype(f32).T.astype(bf16)

    def store(j):
        for b in range(BW):

            @pl.when(j == b)
            def _():
                for half, out in enumerate((key_sum, value_sum)):
                    side = slice(half * ROWS + b * BLK, half * ROWS + (b + 1) * BLK)
                    out[b * BLK : (b + 1) * BLK] = (
                        terms[half * BLK : (half + 1) * BLK].astype(f32)
                        + chip_back[side].astype(f32)
                        + cross_back[side].astype(f32)
                    )

    backward_over(
        own_slots(key, value), seen, query, upward, stat, query_t, held, place, terms, store
    )
    for pair in range(PAIRS):
        query_grad[:, feature(pair)] = (query_t[pair] * SCALE).T.astype(bf16)


def first_sum_kernel(far2, pick, key_near, value_near, key_sum, value_sum):
    for half, (near, out) in enumerate(((key_near, key_sum), (value_near, value_sum))):
        far_part = far2[half * BLK : (half + 1) * BLK].astype(f32)
        for b in range(BW):
            rows = slice(b * BLK, (b + 1) * BLK)
            out[rows] = near[rows] + jnp.where(pick[0, 2] == b, far_part, 0.0)


def second_sum_kernel(pick, key_sum, value_sum, far0, far1, low_block, high_block, key_grad, value_grad):
    for half, (near, out) in enumerate(((key_sum, key_grad), (value_sum, value_grad))):
        part = slice(half * BLK, (half + 1) * BLK)
        for b in range(BW):
            rows = slice(b * BLK, (b + 1) * BLK)
            total = near[rows]
            if b == 0:
                total = total + low_block[part].astype(f32)
            if b == BW - 1:
                total = total + high_block[part].astype(f32)
            for slot, far in enumerate((far0, far1)):
                total = total + jnp.where(pick[0, slot] == b, far[part].astype(f32), 0.0)
            out[rows] = total.astype(bf16)


def call(kernel, shapes, specs, args, scratch=(), outs=None, cost=None):
    return pl.pallas_call(
        kernel,
        out_shape=shapes,
        in_specs=specs,
        out_specs=outs if outs is not None else jax.tree.map(lambda _: vmem(), shapes),
        scratch_shapes=list(scratch),
        compiler_params=pltpu.CompilerParams(vmem_limit_bytes=VMEM_LIMIT),
        cost_estimate=cost,
    )(*args)


def shape(dims, dtype):
    return jax.ShapeDtypeStruct(dims, dtype)


def hbm():
    return pl.BlockSpec(memory_space=pl.ANY)


STATE = [shape((PAIRS, 8, ROWS), f32), shape((PAIRS, BLK, ROWS), f32)]
RIM = shape((2 * BLK, D), bf16)
SIDE = shape((2 * ROWS, D), bf16)


def block_of(key, value, start, out):
    rows = pl.ds(pl.multiple_of(start, BLK), BLK)
    out[0:BLK] = key[rows]
    out[BLK : 2 * BLK] = value[rows]


def pack_first_kernel(pick, key, value, far2, whole):
    block_of(key, value, pick[0, 2] * BLK, far2)
    whole[0:ROWS] = key[...]
    whole[ROWS : 2 * ROWS] = value[...]


def pack_rest_kernel(pick, chip, cross, key, value, right, left, far0, far1):
    block_of(key, value, 0, right)
    block_of(key, value, ROWS - BLK, left)
    block_of(key, value, pick[0, 0] * BLK, far0)
    block_of(key, value, pick[0, 1] * BLK, far1)


def pack_first(pick, key, value):
    return call(pack_first_kernel, [RIM, SIDE], [smem(), vmem(), vmem()], (pick, key, value))


def pack_rest(pick, chip, cross, key, value):
    return call(
        pack_rest_kernel,
        [RIM] * 4,
        [smem(), hbm(), hbm(), vmem(), vmem()],
        (pick, chip, cross, key, value),
    )


def seen_scratch(slots):
    return [pltpu.VMEM((slots, 2 * BLK, D), bf16), pltpu.SMEM((16,), jnp.int32)]


def run_first(plan, queries, upstream, *near):
    return call(
        first_kernel,
        STATE + [shape((PAIRS, BLK, ROWS), f32)],
        [smem()] + [vmem()] * 6,
        (plan, queries, upstream, *near),
        scratch=seen_scratch(6),
    )


def run_far(far2, plan, queries, stat, acc):
    return call(
        far_kernel,
        STATE,
        [vmem(), smem()] + [vmem()] * 3,
        (far2, plan, queries, stat, acc),
        scratch=seen_scratch(1),
    )


def run_middle(far2, plan, *rest):
    return call(
        middle_kernel,
        [STATE[0], shape((PAIRS, BLK, ROWS), bf16), STATE[1], RIM, SIDE, SIDE],
        [vmem(), smem()] + [vmem()] * 11,
        (far2, plan, *rest),
        scratch=[pltpu.VMEM((PAIRS, BLK, ROWS), f32), pltpu.VMEM((2 * BLK, D), bf16)]
        + seen_scratch(5),
    )


def run_rest(plan, *rest):
    return call(
        rest_kernel,
        [RIM] * 4 + [STATE[1]],
        [smem()] + [vmem()] * 6 + [hbm()] * 2 + [vmem()] * 2,
        (plan, *rest),
        scratch=[pltpu.VMEM((2 * BLK, D), bf16)] + seen_scratch(4),
    )


def run_own(plan, *rest):
    whole = shape((ROWS, D), bf16)
    total = shape((ROWS, D), f32)
    return call(
        own_kernel,
        [whole, whole, total, total],
        [smem()] + [vmem()] * 9,
        (plan, *rest),
        scratch=[pltpu.VMEM((PAIRS, BLK, ROWS), f32), pltpu.VMEM((2 * BLK, D), bf16)]
        + seen_scratch(2),
    )


def run_first_sum(far2, pick, *rest):
    whole = shape((ROWS, D), f32)
    return call(
        first_sum_kernel, [whole, whole], [vmem(), smem()] + [vmem()] * 2, (far2, pick, *rest)
    )


def run_second_sum(pick, *rest):
    whole = shape((ROWS, D), bf16)
    return call(second_sum_kernel, [whole, whole], [smem()] + [vmem()] * 6, (pick, *rest))


def sides(chip, cross):
    count = lax.axis_size("narrow")
    across = [(i, i + 1) for i in range(1, count - 1, 2)]
    return (
        lax.ppermute(chip, "narrow", [(i, i ^ 1) for i in range(count)]),
        lax.ppermute(cross, "narrow", across + [(b, a) for a, b in across]),
    )


def partner(value, distance):
    mask = 2**distance
    return lax.ppermute(value, "wide", [(s, s ^ mask) for s in range(lax.axis_size("wide"))])


def shift(value, axis, step):
    count = lax.axis_size(axis)
    pairs = [(s, s + step) for s in range(count) if 0 <= s + step < count]
    return lax.ppermute(value, axis, pairs)


def on_device(queries, key_rows, value_rows, upstream, pattern, expander_pick):
    wide_total = lax.axis_size("wide")
    narrow_total = lax.axis_size("narrow")
    wide_pos = lax.axis_index("wide")
    narrow_pos = lax.axis_index("narrow")
    top_bit = wide_total.bit_length() - 1

    even = narrow_pos & 1 == 0
    near_side = jnp.where(even, pattern[:, 6:8], pattern[:, 4:6])
    far_side = jnp.where(even, pattern[:, 4:6], pattern[:, 6:8])
    inner = (narrow_pos > 0) & (narrow_pos < narrow_total - 1)
    plan = jnp.concatenate(
        [
            pattern[:, 0:2],
            jnp.where(wide_pos > 0, pattern[:, 2:3], 0),
            jnp.where(wide_pos < wide_total - 1, pattern[:, 3:4], 0),
            near_side,
            jnp.where(inner, far_side, 0),
            pattern[:, 8:],
        ],
        axis=1,
    )

    far2_pair, whole = pack_first(expander_pick, key_rows, value_rows)
    chip, cross = sides(whole, whole)
    far2 = partner(far2_pair, top_bit - EXP)
    right_pair, left_pair, far0_pair, far1_pair = pack_rest(
        expander_pick, chip, cross, key_rows, value_rows
    )
    rest = (
        shift(left_pair, "wide", 1),
        shift(right_pair, "wide", -1),
        partner(far0_pair, top_bit - 1),
        partner(far1_pair, top_bit - 2),
    )
    stat, acc, upward_t = run_first(plan, queries, upstream, key_rows, value_rows, chip, cross)
    stat, acc = run_far(far2, plan, queries, stat, acc)
    stat, out_t, query_t, far2_term, chip_term, cross_term = run_middle(
        far2, plan, queries, upstream, chip, cross, *rest, stat, acc, upward_t
    )
    far2_back = partner(far2_term, top_bit - EXP)
    back = sides(chip_term, cross_term)
    left_term, right_term, far0_term, far1_term, query_t = run_rest(
        plan, queries, upstream, *rest, *back, stat, query_t
    )
    attention, query_grad, key_near, value_near = run_own(
        plan, queries, upstream, key_rows, value_rows, *back, stat, out_t, query_t
    )
    key_sum, value_sum = run_first_sum(far2_back, expander_pick, key_near, value_near)
    key_grad, value_grad = run_second_sum(
        expander_pick,
        key_sum,
        value_sum,
        partner(far0_term, top_bit - 1),
        partner(far1_term, top_bit - 2),
        shift(right_term, "wide", 1),
        shift(left_term, "wide", -1),
    )
    return (attention, query_grad, key_grad, value_grad)


def solution(mesh):
    placed = P(("wide", "narrow"), None)
    return jax.shard_map(
        on_device,
        mesh=mesh,
        in_specs=(placed,) * 6,
        out_specs=(placed,) * 4,
        check_vma=False,
    )
```

```python
import jax
import jax.numpy as jnp
from jax import lax
from jax.experimental import pallas as pl
from jax.experimental.pallas import tpu as pltpu
from jax.sharding import PartitionSpec as P

D = 768
HD = 64
BLK = 128
BW = 2
EXP = 3
ROWS = BW * BLK
PAIRS = D // BLK
GROUP = 6
SCALE = HD ** (-0.5)
LOG2 = SCALE * 1.4426950408889634
HIDDEN = -1e30

VMEM_LIMIT = 24 * 1024 * 1024
NT = (((1,), (1,)), ((), ()))
NN = (((1,), (0,)), ((), ()))
f32 = jnp.float32
bf16 = jnp.bfloat16


def vmem():
    return pl.BlockSpec(memory_space=pltpu.VMEM)


def smem():
    return pl.BlockSpec(memory_space=pltpu.SMEM)


def dot(a, b, dims):
    return lax.dot_general(a, b, dims, preferred_element_type=f32)


def lanes(pair):
    return pl.ds(pl.multiple_of(pair * BLK, BLK), BLK)


def low_lane(shape):
    return lax.broadcasted_iota(jnp.int32, shape, 1) < HD


def low_row(shape):
    return lax.broadcasted_iota(jnp.int32, shape, 0) < HD


def stacked(tile):
    low = low_lane(tile.shape)
    zero = jnp.zeros_like(tile)
    return jnp.concatenate([jnp.where(low, tile, zero), jnp.where(low, zero, tile)], axis=0)


def stacked_t(tile):
    turned = tile.astype(f32).T
    low = low_row(turned.shape)
    zero = jnp.zeros_like(turned)
    return jnp.concatenate(
        [jnp.where(low, turned, zero), jnp.where(low, zero, turned)], axis=1
    ).astype(bf16)


def by_head(stat):
    return jnp.concatenate(
        [jnp.broadcast_to(stat[0:1], (BLK, ROWS)), jnp.broadcast_to(stat[1:2], (BLK, ROWS))], axis=0
    )


def by_feature(stat):
    return jnp.concatenate(
        [jnp.broadcast_to(stat[0:1], (HD, ROWS)), jnp.broadcast_to(stat[1:2], (HD, ROWS))], axis=0
    )


def seen_row(seen0, seen1):
    first = lax.broadcasted_iota(jnp.int32, (1, ROWS), 1) < BLK
    return jnp.where(first, seen0, seen1) > 0


def head_reduce(fn, tile):
    half = tile.shape[0] // 2
    return jnp.concatenate(
        [fn(tile[:half], axis=0, keepdims=True), fn(tile[half:], axis=0, keepdims=True)], axis=0
    )


def scores_t(key_tile, query_tile):
    return dot(stacked(key_tile), query_tile, NT)


def online(keys, values, queries, row, stat_ref, acc_ref, pairs):
    scores = [scores_t(k, q) for k, q in zip(keys, queries)]
    turned = [stacked_t(v) for v in values]
    probs, decays = [], []
    for pair, tile in zip(pairs, scores):
        old = stat_ref[pair, 0:2, :]
        new = jnp.where(row, jnp.maximum(old, head_reduce(jnp.max, tile) * LOG2), old)
        decay = jnp.exp2(old - new)
        weight = jnp.exp2(tile * LOG2 - by_head(jnp.where(row, new, -HIDDEN)))
        stat_ref[pair, 0:2, :] = new
        stat_ref[pair, 2:4, :] = stat_ref[pair, 2:4, :] * decay + head_reduce(jnp.sum, weight)
        probs.append(weight.astype(bf16))
        decays.append(decay)
    for i, pair in enumerate(pairs):
        acc_ref[pair] = acc_ref[pair] * by_feature(decays[i]) + dot(turned[i], probs[i], NN)


def own_head(product):
    return jnp.where(low_lane((BLK, BLK)), product[:BLK], product[BLK:])


def backward(keys, values, queries, upwards, row, stats):
    scores = [scores_t(k, q) for k, q in zip(keys, queries)]
    products = [dot(stacked(v), u, NT) for v, u in zip(values, upwards)]
    weights, grads = [], []
    for tile, product, stat in zip(scores, products, stats):
        weight = jnp.exp2(tile * LOG2 - by_head(jnp.where(row, stat[0:2], -HIDDEN)))
        weights.append(weight.astype(bf16))
        grads.append((weight * (product - by_head(stat[2:4]))).astype(bf16))
    value_terms = [own_head(dot(w, u, NN)).astype(bf16) for w, u in zip(weights, upwards)]
    key_terms = [(own_head(dot(g, q, NN)) * SCALE).astype(bf16) for g, q in zip(grads, queries)]
    query_ts = [dot(stacked_t(k), g, NN) for k, g in zip(keys, grads)]
    return key_terms, value_terms, query_ts


def groups():
    return [range(first, first + GROUP) for first in range(0, PAIRS, GROUP)]


def own_slots(whole):
    return [(b, whole, b * BLK, whole, ROWS + b * BLK) for b in range(BW)]


def side_slots(chip, cross):
    return [
        (4 + BW * i + b, ref, b * BLK, ref, ROWS + b * BLK)
        for i, ref in enumerate((chip, cross))
        for b in range(BW)
    ]


def pair_slots(columns, *refs):
    return [(j, ref, 0, ref, BLK) for j, ref in zip(columns, refs)]


def rest_slots(left, right, far0, far1):
    return pair_slots((2, 3, 8, 9), left, right, far0, far1)


def rows_at(start):
    return pl.ds(start if isinstance(start, int) else pl.multiple_of(start, BLK), BLK)


def feature(pair):
    return slice(pair * BLK, (pair + 1) * BLK)


def load_seen(seen, slots, held, place):
    count = jnp.int32(0)
    for j, k_ref, k_row, v_ref, v_row in slots:
        used = seen[0, j] + seen[1, j] > 0
        at = count

        @pl.when(used)
        def _():
            place[at] = j
            held[at, 0:BLK] = k_ref[rows_at(k_row)]
            held[at, BLK : 2 * BLK] = v_ref[rows_at(v_row)]

        count = count + used.astype(jnp.int32)
    return count


def forward_over(slots, seen, query, stat, acc, held, place):
    count = load_seen(seen, slots, held, place)

    def step(at, carry):
        j = place[at]
        row = seen_row(seen[0, j], seen[1, j])
        for pairs in groups():
            online(
                [held[at, 0:BLK, feature(p)] for p in pairs],
                [held[at, BLK : 2 * BLK, feature(p)] for p in pairs],
                [query[:, feature(p)] for p in pairs],
                row,
                stat,
                acc,
                pairs,
            )
        return carry

    lax.fori_loop(0, count, step, 0)


def first_kernel(seen, query, upward, whole, chip, cross, stat, acc, upward_t, held, place):
    for pair in range(PAIRS):
        stat[pair, 0:2, :] = jnp.full((2, ROWS), HIDDEN, f32)
        stat[pair, 2:4, :] = jnp.zeros((2, ROWS), f32)
        acc[pair] = jnp.zeros((BLK, ROWS), f32)
        upward_t[pair] = upward[:, feature(pair)].astype(f32).T
    forward_over(
        own_slots(whole) + side_slots(chip, cross), seen, query, stat, acc, held, place
    )


def far_kernel(far2, seen, query, stat_in, acc_in, stat, acc, held, place):
    stat[...] = stat_in[...]
    acc[...] = acc_in[...]
    forward_over(pair_slots((10,), far2), seen, query, stat, acc, held, place)


def clear_unseen(slots, seen):
    for j, k_ref, k_row, v_ref, v_row in slots:

        @pl.when(seen[0, j] + seen[1, j] == 0)
        def _():
            k_ref[k_row : k_row + BLK] = jnp.zeros((BLK, D), bf16)
            v_ref[v_row : v_row + BLK] = jnp.zeros((BLK, D), bf16)


def backward_over(sources, seen, query, upward, stat, query_t, held, place, terms, store):
    count = load_seen(seen, sources, held, place)

    def step(at, carry):
        j = place[at]
        row = seen_row(seen[0, j], seen[1, j])
        for pairs in groups():
            key_terms, value_terms, grads = backward(
                [held[at, 0:BLK, feature(p)] for p in pairs],
                [held[at, BLK : 2 * BLK, feature(p)] for p in pairs],
                [query[:, feature(p)] for p in pairs],
                [upward[:, feature(p)] for p in pairs],
                row,
                [stat[p] for p in pairs],
            )
            for i, pair in enumerate(pairs):
                terms[0:BLK, feature(pair)] = key_terms[i]
                terms[BLK : 2 * BLK, feature(pair)] = value_terms[i]
                query_t[pair] = query_t[pair] + grads[i]
        store(j)
        return carry

    lax.fori_loop(0, count, step, 0)


def store_terms(slots, terms, j):
    for slot, k_ref, k_row, v_ref, v_row in slots:

        @pl.when(j == slot)
        def _():
            k_ref[k_row : k_row + BLK] = terms[0:BLK]
            v_ref[v_row : v_row + BLK] = terms[BLK : 2 * BLK]


def middle_kernel(
    far2,
    seen,
    query,
    upward,
    chip,
    cross,
    left,
    right,
    far0,
    far1,
    stat_in,
    acc_in,
    upward_t,
    stat,
    out_t,
    query_t,
    far2_term,
    chip_term,
    cross_term,
    acc,
    terms,
    held,
    place,
):
    stat[...] = stat_in[...]
    acc[...] = acc_in[...]
    forward_over(rest_slots(left, right, far0, far1), seen, query, stat, acc, held, place)

    for pair in range(PAIRS):
        total = stat[pair, 2:4, :]
        attended = (acc[pair] * by_feature(1.0 / total)).astype(bf16)
        out_t[pair] = attended
        stat[pair, 0:2, :] = stat[pair, 0:2, :] + jnp.log2(total)
        stat[pair, 2:4, :] = head_reduce(jnp.sum, upward_t[pair] * attended.astype(f32))

    query_t[...] = jnp.zeros_like(query_t)
    targets = pair_slots((10,), far2_term) + side_slots(chip_term, cross_term)
    clear_unseen(targets, seen)
    backward_over(
        pair_slots((10,), far2) + side_slots(chip, cross),
        seen,
        query,
        upward,
        stat,
        query_t,
        held,
        place,
        terms,
        lambda j: store_terms(targets, terms, j),
    )


def terms_kernel(columns, gates):
    def kernel(seen, query, upward, one, two, stat, query_t_in, *refs):
        one_term, two_term, query_t, terms, held, place = refs[gates:]
        query_t[...] = query_t_in[...]
        targets = pair_slots(columns, one_term, two_term)
        clear_unseen(targets, seen)
        backward_over(
            pair_slots(columns, one, two),
            seen,
            query,
            upward,
            stat,
            query_t,
            held,
            place,
            terms,
            lambda j: store_terms(targets, terms, j),
        )

    return kernel


def own_kernel(
    seen,
    query,
    upward,
    whole,
    chip_back,
    cross_back,
    stat,
    out_t,
    query_t_in,
    attention,
    query_grad,
    key_sum,
    value_sum,
    query_t,
    terms,
    held,
    place,
):
    query_t[...] = query_t_in[...]
    for pair in range(PAIRS):
        attention[:, feature(pair)] = out_t[pair].astype(f32).T.astype(bf16)

    def store(j):
        for b in range(BW):

            @pl.when(j == b)
            def _():
                for half, out in enumerate((key_sum, value_sum)):
                    side = slice(half * ROWS + b * BLK, half * ROWS + (b + 1) * BLK)
                    out[b * BLK : (b + 1) * BLK] = (
                        terms[half * BLK : (half + 1) * BLK].astype(f32)
                        + chip_back[side].astype(f32)
                        + cross_back[side].astype(f32)
                    )

    backward_over(
        own_slots(whole), seen, query, upward, stat, query_t, held, place, terms, store
    )
    for pair in range(PAIRS):
        query_grad[:, feature(pair)] = (query_t[pair] * SCALE).T.astype(bf16)


def first_sum_kernel(far2, pick, key_near, value_near, key_sum, value_sum):
    for half, (near, out) in enumerate(((key_near, key_sum), (value_near, value_sum))):
        far_part = far2[half * BLK : (half + 1) * BLK].astype(f32)
        for b in range(BW):
            rows = slice(b * BLK, (b + 1) * BLK)
            out[rows] = near[rows] + jnp.where(pick[0, 2] == b, far_part, 0.0)


def second_sum_kernel(pick, key_sum, value_sum, low_block, high_block, far0, far1, key_grad, value_grad):
    for half, (near, out) in enumerate(((key_sum, key_grad), (value_sum, value_grad))):
        part = slice(half * BLK, (half + 1) * BLK)
        for b in range(BW):
            rows = slice(b * BLK, (b + 1) * BLK)
            total = near[rows]
            if b == 0:
                total = total + low_block[part].astype(f32)
            if b == BW - 1:
                total = total + high_block[part].astype(f32)
            for slot, far in enumerate((far0, far1)):
                total = total + jnp.where(pick[0, slot] == b, far[part].astype(f32), 0.0)
            out[rows] = total.astype(bf16)


def call(kernel, shapes, specs, args, scratch=(), outs=None, cost=None):
    return pl.pallas_call(
        kernel,
        out_shape=shapes,
        in_specs=specs,
        out_specs=outs if outs is not None else jax.tree.map(lambda _: vmem(), shapes),
        scratch_shapes=list(scratch),
        compiler_params=pltpu.CompilerParams(vmem_limit_bytes=VMEM_LIMIT),
        cost_estimate=cost,
    )(*args)


def shape(dims, dtype):
    return jax.ShapeDtypeStruct(dims, dtype)


def hbm():
    return pl.BlockSpec(memory_space=pl.ANY)


STATE = [shape((PAIRS, 8, ROWS), f32), shape((PAIRS, BLK, ROWS), f32)]
RIM = shape((2 * BLK, D), bf16)
SIDE = shape((2 * ROWS, D), bf16)


def block_of(whole, start, out):
    for half in range(2):
        rows = pl.ds(pl.multiple_of(half * ROWS + start, BLK), BLK)
        out[half * BLK : (half + 1) * BLK] = whole[rows]


def pack_first_kernel(pick, key, value, whole, far2, right, left):
    whole[0:ROWS] = key[...]
    whole[ROWS : 2 * ROWS] = value[...]
    block_of(whole, pick[0, 2] * BLK, far2)
    block_of(whole, 0, right)
    block_of(whole, ROWS - BLK, left)


def pack_rest_kernel(pick, chip, cross, whole, far0, far1):
    block_of(whole, pick[0, 0] * BLK, far0)
    block_of(whole, pick[0, 1] * BLK, far1)


def pack_first(pick, key, value):
    return call(
        pack_first_kernel, [SIDE, RIM, RIM, RIM], [smem(), vmem(), vmem()], (pick, key, value)
    )


def pack_rest(pick, chip, cross, whole):
    return call(
        pack_rest_kernel,
        [RIM] * 2,
        [smem(), hbm(), hbm(), vmem()],
        (pick, chip, cross, whole),
    )


def seen_scratch(slots):
    return [pltpu.VMEM((slots, 2 * BLK, D), bf16), pltpu.SMEM((16,), jnp.int32)]


def run_first(plan, *rest):
    return call(
        first_kernel,
        STATE + [shape((PAIRS, BLK, ROWS), f32)],
        [smem()] + [vmem()] * 5,
        (plan, *rest),
        scratch=seen_scratch(6),
    )


def run_far(far2, plan, queries, stat, acc):
    return call(
        far_kernel,
        STATE,
        [vmem(), smem()] + [vmem()] * 3,
        (far2, plan, queries, stat, acc),
        scratch=seen_scratch(1),
    )


def run_middle(far2, plan, *rest):
    return call(
        middle_kernel,
        [STATE[0], shape((PAIRS, BLK, ROWS), bf16), STATE[1], RIM, SIDE, SIDE],
        [vmem(), smem()] + [vmem()] * 11,
        (far2, plan, *rest),
        scratch=[pltpu.VMEM((PAIRS, BLK, ROWS), f32), pltpu.VMEM((2 * BLK, D), bf16)]
        + seen_scratch(5),
    )


def run_terms(columns, plan, queries, upstream, one, two, stat, query_t, *gates):
    return call(
        terms_kernel(columns, len(gates)),
        [RIM, RIM, STATE[1]],
        [smem()] + [vmem()] * 6 + [hbm()] * len(gates),
        (plan, queries, upstream, one, two, stat, query_t, *gates),
        scratch=[pltpu.VMEM((2 * BLK, D), bf16)] + seen_scratch(2),
    )


def run_own(plan, *rest):
    whole = shape((ROWS, D), bf16)
    total = shape((ROWS, D), f32)
    return call(
        own_kernel,
        [whole, whole, total, total],
        [smem()] + [vmem()] * 8,
        (plan, *rest),
        scratch=[pltpu.VMEM((PAIRS, BLK, ROWS), f32), pltpu.VMEM((2 * BLK, D), bf16)]
        + seen_scratch(2),
    )


def run_first_sum(far2, pick, *rest):
    whole = shape((ROWS, D), f32)
    return call(
        first_sum_kernel, [whole, whole], [vmem(), smem()] + [vmem()] * 2, (far2, pick, *rest)
    )


def run_second_sum(pick, *rest):
    whole = shape((ROWS, D), bf16)
    return call(second_sum_kernel, [whole, whole], [smem()] + [vmem()] * 6, (pick, *rest))


def sides(chip, cross):
    count = lax.axis_size("narrow")
    across = [(i, i + 1) for i in range(1, count - 1, 2)]
    return (
        lax.ppermute(chip, "narrow", [(i, i ^ 1) for i in range(count)]),
        lax.ppermute(cross, "narrow", across + [(b, a) for a, b in across]),
    )


def partner(value, distance):
    mask = 2**distance
    return lax.ppermute(value, "wide", [(s, s ^ mask) for s in range(lax.axis_size("wide"))])


def shift(value, axis, step):
    count = lax.axis_size(axis)
    pairs = [(s, s + step) for s in range(count) if 0 <= s + step < count]
    return lax.ppermute(value, axis, pairs)


def on_device(queries, key_rows, value_rows, upstream, pattern, expander_pick):
    wide_total = lax.axis_size("wide")
    narrow_total = lax.axis_size("narrow")
    wide_pos = lax.axis_index("wide")
    narrow_pos = lax.axis_index("narrow")
    top_bit = wide_total.bit_length() - 1

    even = narrow_pos & 1 == 0
    near_side = jnp.where(even, pattern[:, 6:8], pattern[:, 4:6])
    far_side = jnp.where(even, pattern[:, 4:6], pattern[:, 6:8])
    inner = (narrow_pos > 0) & (narrow_pos < narrow_total - 1)
    plan = jnp.concatenate(
        [
            pattern[:, 0:2],
            jnp.where(wide_pos > 0, pattern[:, 2:3], 0),
            jnp.where(wide_pos < wide_total - 1, pattern[:, 3:4], 0),
            near_side,
            jnp.where(inner, far_side, 0),
            pattern[:, 8:],
        ],
        axis=1,
    )

    whole, far2_pair, right_pair, left_pair = pack_first(expander_pick, key_rows, value_rows)
    chip, cross = sides(whole, whole)
    far2 = partner(far2_pair, top_bit - EXP)
    left = shift(left_pair, "wide", 1)
    right = shift(right_pair, "wide", -1)
    far0_pair, far1_pair = pack_rest(expander_pick, chip, cross, whole)
    far0 = partner(far0_pair, top_bit - 1)
    far1 = partner(far1_pair, top_bit - 2)
    stat, acc, upward_t = run_first(plan, queries, upstream, whole, chip, cross)
    stat, acc = run_far(far2, plan, queries, stat, acc)
    stat, out_t, query_t, far2_term, chip_term, cross_term = run_middle(
        far2, plan, queries, upstream, chip, cross, left, right, far0, far1, stat, acc, upward_t
    )
    far2_back = partner(far2_term, top_bit - EXP)
    back = sides(chip_term, cross_term)
    left_term, right_term, query_t = run_terms(
        (2, 3), plan, queries, upstream, left, right, stat, query_t
    )
    far0_term, far1_term, query_t = run_terms(
        (8, 9), plan, queries, upstream, far0, far1, stat, query_t, *back
    )
    attention, query_grad, key_near, value_near = run_own(
        plan, queries, upstream, whole, *back, stat, out_t, query_t
    )
    key_sum, value_sum = run_first_sum(far2_back, expander_pick, key_near, value_near)
    key_grad, value_grad = run_second_sum(
        expander_pick,
        key_sum,
        value_sum,
        shift(right_term, "wide", 1),
        shift(left_term, "wide", -1),
        partner(far0_term, top_bit - 1),
        partner(far1_term, top_bit - 2),
    )
    return (attention, query_grad, key_grad, value_grad)


def solution(mesh):
    placed = P(("wide", "narrow"), None)
    return jax.shard_map(
        on_device,
        mesh=mesh,
        in_specs=(placed,) * 6,
        out_specs=(placed,) * 4,
        check_vma=False,
    )
```

```python
import jax
import jax.numpy as jnp
from jax import lax
from jax.experimental import pallas as pl
from jax.experimental.pallas import tpu as pltpu
from jax.sharding import PartitionSpec as P

D = 768
HD = 64
BLK = 128
BW = 2
EXP = 3
ROWS = BW * BLK
PAIRS = D // BLK
GROUP = 6
SCALE = HD ** (-0.5)
LOG2 = SCALE * 1.4426950408889634
HIDDEN = -1e30

VMEM_LIMIT = 24 * 1024 * 1024
NT = (((1,), (1,)), ((), ()))
NN = (((1,), (0,)), ((), ()))
f32 = jnp.float32
bf16 = jnp.bfloat16


def vmem():
    return pl.BlockSpec(memory_space=pltpu.VMEM)


def smem():
    return pl.BlockSpec(memory_space=pltpu.SMEM)


def dot(a, b, dims):
    return lax.dot_general(a, b, dims, preferred_element_type=f32)


def lanes(pair):
    return pl.ds(pl.multiple_of(pair * BLK, BLK), BLK)


def low_lane(shape):
    return lax.broadcasted_iota(jnp.int32, shape, 1) < HD


def low_row(shape):
    return lax.broadcasted_iota(jnp.int32, shape, 0) < HD


def stacked(tile):
    low = low_lane(tile.shape)
    zero = jnp.zeros_like(tile)
    return jnp.concatenate([jnp.where(low, tile, zero), jnp.where(low, zero, tile)], axis=0)


def stacked_t(tile):
    turned = tile.astype(f32).T
    low = low_row(turned.shape)
    zero = jnp.zeros_like(turned)
    return jnp.concatenate(
        [jnp.where(low, turned, zero), jnp.where(low, zero, turned)], axis=1
    ).astype(bf16)


def by_head(stat):
    return jnp.concatenate(
        [jnp.broadcast_to(stat[0:1], (BLK, ROWS)), jnp.broadcast_to(stat[1:2], (BLK, ROWS))], axis=0
    )


def by_feature(stat):
    return jnp.concatenate(
        [jnp.broadcast_to(stat[0:1], (HD, ROWS)), jnp.broadcast_to(stat[1:2], (HD, ROWS))], axis=0
    )


def seen_row(seen0, seen1):
    first = lax.broadcasted_iota(jnp.int32, (1, ROWS), 1) < BLK
    return jnp.where(first, seen0, seen1) > 0


def head_reduce(fn, tile):
    half = tile.shape[0] // 2
    return jnp.concatenate(
        [fn(tile[:half], axis=0, keepdims=True), fn(tile[half:], axis=0, keepdims=True)], axis=0
    )


def scores_t(key_tile, query_tile):
    return dot(stacked(key_tile), query_tile, NT)


def online(keys, values, queries, row, stat_ref, acc_ref, pairs):
    scores = [scores_t(k, q) for k, q in zip(keys, queries)]
    turned = [stacked_t(v) for v in values]
    probs, decays = [], []
    for pair, tile in zip(pairs, scores):
        old = stat_ref[pair, 0:2, :]
        new = jnp.where(row, jnp.maximum(old, head_reduce(jnp.max, tile) * LOG2), old)
        decay = jnp.exp2(old - new)
        weight = jnp.exp2(tile * LOG2 - by_head(jnp.where(row, new, -HIDDEN)))
        stat_ref[pair, 0:2, :] = new
        stat_ref[pair, 2:4, :] = stat_ref[pair, 2:4, :] * decay + head_reduce(jnp.sum, weight)
        probs.append(weight.astype(bf16))
        decays.append(decay)
    for i, pair in enumerate(pairs):
        acc_ref[pair] = acc_ref[pair] * by_feature(decays[i]) + dot(turned[i], probs[i], NN)


def own_head(product):
    return jnp.where(low_lane((BLK, BLK)), product[:BLK], product[BLK:])


def backward(keys, values, queries, upwards, row, stats):
    scores = [scores_t(k, q) for k, q in zip(keys, queries)]
    products = [dot(stacked(v), u, NT) for v, u in zip(values, upwards)]
    weights, grads = [], []
    for tile, product, stat in zip(scores, products, stats):
        weight = jnp.exp2(tile * LOG2 - by_head(jnp.where(row, stat[0:2], -HIDDEN)))
        weights.append(weight.astype(bf16))
        grads.append((weight * (product - by_head(stat[2:4]))).astype(bf16))
    value_terms = [own_head(dot(w, u, NN)).astype(bf16) for w, u in zip(weights, upwards)]
    key_terms = [(own_head(dot(g, q, NN)) * SCALE).astype(bf16) for g, q in zip(grads, queries)]
    query_ts = [dot(stacked_t(k), g, NN) for k, g in zip(keys, grads)]
    return key_terms, value_terms, query_ts


def groups():
    return [range(first, first + GROUP) for first in range(0, PAIRS, GROUP)]


def own_slots(whole):
    return [(b, whole, b * BLK, whole, ROWS + b * BLK) for b in range(BW)]


def side_slots(chip, cross):
    return [
        (4 + BW * i + b, ref, b * BLK, ref, ROWS + b * BLK)
        for i, ref in enumerate((chip, cross))
        for b in range(BW)
    ]


def pair_slots(columns, *refs):
    return [(j, ref, 0, ref, BLK) for j, ref in zip(columns, refs)]


def rest_slots(left, right, far0, far1):
    return pair_slots((2, 3, 8, 9), left, right, far0, far1)


def rows_at(start):
    return pl.ds(start if isinstance(start, int) else pl.multiple_of(start, BLK), BLK)


def feature(pair):
    return slice(pair * BLK, (pair + 1) * BLK)


def load_seen(seen, slots, held, place):
    count = jnp.int32(0)
    for j, k_ref, k_row, v_ref, v_row in slots:
        used = seen[0, j] + seen[1, j] > 0
        at = count

        @pl.when(used)
        def _():
            place[at] = j
            held[at, 0:BLK] = k_ref[rows_at(k_row)]
            held[at, BLK : 2 * BLK] = v_ref[rows_at(v_row)]

        count = count + used.astype(jnp.int32)
    return count


def forward_over(slots, seen, query, stat, acc, held, place):
    count = load_seen(seen, slots, held, place)

    def step(at, carry):
        j = place[at]
        row = seen_row(seen[0, j], seen[1, j])
        for pairs in groups():
            online(
                [held[at, 0:BLK, feature(p)] for p in pairs],
                [held[at, BLK : 2 * BLK, feature(p)] for p in pairs],
                [query[:, feature(p)] for p in pairs],
                row,
                stat,
                acc,
                pairs,
            )
        return carry

    lax.fori_loop(0, count, step, 0)


def first_kernel(seen, query, upward, whole, chip, cross, stat, acc, upward_t, held, place):
    for pair in range(PAIRS):
        stat[pair, 0:2, :] = jnp.full((2, ROWS), HIDDEN, f32)
        stat[pair, 2:4, :] = jnp.zeros((2, ROWS), f32)
        acc[pair] = jnp.zeros((BLK, ROWS), f32)
        upward_t[pair] = upward[:, feature(pair)].astype(f32).T
    forward_over(
        own_slots(whole) + side_slots(chip, cross), seen, query, stat, acc, held, place
    )


def far_kernel(far2, seen, query, stat_in, acc_in, stat, acc, held, place):
    stat[...] = stat_in[...]
    acc[...] = acc_in[...]
    forward_over(pair_slots((10,), far2), seen, query, stat, acc, held, place)


def clear_unseen(slots, seen):
    for j, k_ref, k_row, v_ref, v_row in slots:

        @pl.when(seen[0, j] + seen[1, j] == 0)
        def _():
            k_ref[k_row : k_row + BLK] = jnp.zeros((BLK, D), bf16)
            v_ref[v_row : v_row + BLK] = jnp.zeros((BLK, D), bf16)


def backward_over(sources, seen, query, upward, stat, query_t, held, place, terms, store):
    count = load_seen(seen, sources, held, place)

    def step(at, carry):
        j = place[at]
        row = seen_row(seen[0, j], seen[1, j])
        for pairs in groups():
            key_terms, value_terms, grads = backward(
                [held[at, 0:BLK, feature(p)] for p in pairs],
                [held[at, BLK : 2 * BLK, feature(p)] for p in pairs],
                [query[:, feature(p)] for p in pairs],
                [upward[:, feature(p)] for p in pairs],
                row,
                [stat[p] for p in pairs],
            )
            for i, pair in enumerate(pairs):
                terms[0:BLK, feature(pair)] = key_terms[i]
                terms[BLK : 2 * BLK, feature(pair)] = value_terms[i]
                query_t[pair] = query_t[pair] + grads[i]
        store(j)
        return carry

    lax.fori_loop(0, count, step, 0)


def store_terms(slots, terms, j):
    for slot, k_ref, k_row, v_ref, v_row in slots:

        @pl.when(j == slot)
        def _():
            k_ref[k_row : k_row + BLK] = terms[0:BLK]
            v_ref[v_row : v_row + BLK] = terms[BLK : 2 * BLK]


def middle_kernel(
    far2,
    seen,
    query,
    upward,
    chip,
    cross,
    far0,
    far1,
    left,
    right,
    stat_in,
    acc_in,
    upward_t,
    stat,
    out_t,
    query_t,
    far2_term,
    chip_term,
    cross_term,
    acc,
    terms,
    held,
    place,
):
    stat[...] = stat_in[...]
    acc[...] = acc_in[...]
    forward_over(rest_slots(left, right, far0, far1), seen, query, stat, acc, held, place)

    for pair in range(PAIRS):
        total = stat[pair, 2:4, :]
        attended = (acc[pair] * by_feature(1.0 / total)).astype(bf16)
        out_t[pair] = attended
        stat[pair, 0:2, :] = stat[pair, 0:2, :] + jnp.log2(total)
        stat[pair, 2:4, :] = head_reduce(jnp.sum, upward_t[pair] * attended.astype(f32))

    query_t[...] = jnp.zeros_like(query_t)
    targets = pair_slots((10,), far2_term) + side_slots(chip_term, cross_term)
    clear_unseen(targets, seen)
    backward_over(
        pair_slots((10,), far2) + side_slots(chip, cross),
        seen,
        query,
        upward,
        stat,
        query_t,
        held,
        place,
        terms,
        lambda j: store_terms(targets, terms, j),
    )


def rest_kernel(
    seen,
    query,
    upward,
    left,
    right,
    far0,
    far1,
    chip_back,
    cross_back,
    stat,
    query_t_in,
    left_term,
    right_term,
    far0_term,
    far1_term,
    query_t,
    terms,
    held,
    place,
):
    query_t[...] = query_t_in[...]
    targets = rest_slots(left_term, right_term, far0_term, far1_term)
    clear_unseen(targets, seen)
    backward_over(
        rest_slots(left, right, far0, far1),
        seen,
        query,
        upward,
        stat,
        query_t,
        held,
        place,
        terms,
        lambda j: store_terms(targets, terms, j),
    )


def own_kernel(
    seen,
    query,
    upward,
    whole,
    chip_back,
    cross_back,
    stat,
    out_t,
    query_t_in,
    attention,
    query_grad,
    key_sum,
    value_sum,
    query_t,
    terms,
    held,
    place,
):
    query_t[...] = query_t_in[...]
    for pair in range(PAIRS):
        attention[:, feature(pair)] = out_t[pair].astype(f32).T.astype(bf16)

    def store(j):
        for b in range(BW):

            @pl.when(j == b)
            def _():
                for half, out in enumerate((key_sum, value_sum)):
                    side = slice(half * ROWS + b * BLK, half * ROWS + (b + 1) * BLK)
                    out[b * BLK : (b + 1) * BLK] = (
                        terms[half * BLK : (half + 1) * BLK].astype(f32)
                        + chip_back[side].astype(f32)
                        + cross_back[side].astype(f32)
                    )

    backward_over(
        own_slots(whole), seen, query, upward, stat, query_t, held, place, terms, store
    )
    for pair in range(PAIRS):
        query_grad[:, feature(pair)] = (query_t[pair] * SCALE).T.astype(bf16)


def first_sum_kernel(far2, pick, key_near, value_near, key_sum, value_sum):
    for half, (near, out) in enumerate(((key_near, key_sum), (value_near, value_sum))):
        far_part = far2[half * BLK : (half + 1) * BLK].astype(f32)
        for b in range(BW):
            rows = slice(b * BLK, (b + 1) * BLK)
            out[rows] = near[rows] + jnp.where(pick[0, 2] == b, far_part, 0.0)


def second_sum_kernel(pick, key_sum, value_sum, far0, far1, low_block, high_block, key_grad, value_grad):
    for half, (near, out) in enumerate(((key_sum, key_grad), (value_sum, value_grad))):
        part = slice(half * BLK, (half + 1) * BLK)
        for b in range(BW):
            rows = slice(b * BLK, (b + 1) * BLK)
            total = near[rows]
            if b == 0:
                total = total + low_block[part].astype(f32)
            if b == BW - 1:
                total = total + high_block[part].astype(f32)
            for slot, far in enumerate((far0, far1)):
                total = total + jnp.where(pick[0, slot] == b, far[part].astype(f32), 0.0)
            out[rows] = total.astype(bf16)


def call(kernel, shapes, specs, args, scratch=(), outs=None, cost=None):
    return pl.pallas_call(
        kernel,
        out_shape=shapes,
        in_specs=specs,
        out_specs=outs if outs is not None else jax.tree.map(lambda _: vmem(), shapes),
        scratch_shapes=list(scratch),
        compiler_params=pltpu.CompilerParams(vmem_limit_bytes=VMEM_LIMIT),
        cost_estimate=cost,
    )(*args)


def shape(dims, dtype):
    return jax.ShapeDtypeStruct(dims, dtype)


def hbm():
    return pl.BlockSpec(memory_space=pl.ANY)


STATE = [shape((PAIRS, 8, ROWS), f32), shape((PAIRS, BLK, ROWS), f32)]
RIM = shape((2 * BLK, D), bf16)
SIDE = shape((2 * ROWS, D), bf16)


def block_of(whole, start, out):
    for half in range(2):
        rows = pl.ds(pl.multiple_of(half * ROWS + start, BLK), BLK)
        out[half * BLK : (half + 1) * BLK] = whole[rows]


def pack_first_kernel(pick, key, value, far2, whole):
    whole[0:ROWS] = key[...]
    whole[ROWS : 2 * ROWS] = value[...]
    block_of(whole, pick[0, 2] * BLK, far2)


def pack_rest_kernel(pick, chip, cross, whole, right, left, far0, far1):
    block_of(whole, 0, right)
    block_of(whole, ROWS - BLK, left)
    block_of(whole, pick[0, 0] * BLK, far0)
    block_of(whole, pick[0, 1] * BLK, far1)


def pack_first(pick, key, value):
    return call(pack_first_kernel, [RIM, SIDE], [smem(), vmem(), vmem()], (pick, key, value))


def pack_rest(pick, chip, cross, whole):
    return call(
        pack_rest_kernel, [RIM] * 4, [smem(), hbm(), hbm(), vmem()], (pick, chip, cross, whole)
    )


def seen_scratch(slots):
    return [pltpu.VMEM((slots, 2 * BLK, D), bf16), pltpu.SMEM((16,), jnp.int32)]


def run_first(plan, *rest):
    return call(
        first_kernel,
        STATE + [shape((PAIRS, BLK, ROWS), f32)],
        [smem()] + [vmem()] * 5,
        (plan, *rest),
        scratch=seen_scratch(6),
    )


def run_far(far2, plan, queries, stat, acc):
    return call(
        far_kernel,
        STATE,
        [vmem(), smem()] + [vmem()] * 3,
        (far2, plan, queries, stat, acc),
        scratch=seen_scratch(1),
    )


def run_middle(far2, plan, *rest):
    return call(
        middle_kernel,
        [STATE[0], shape((PAIRS, BLK, ROWS), bf16), STATE[1], RIM, SIDE, SIDE],
        [vmem(), smem()] + [vmem()] * 11,
        (far2, plan, *rest),
        scratch=[pltpu.VMEM((PAIRS, BLK, ROWS), f32), pltpu.VMEM((2 * BLK, D), bf16)]
        + seen_scratch(5),
    )


def run_rest(plan, *rest):
    return call(
        rest_kernel,
        [RIM] * 4 + [STATE[1]],
        [smem()] + [vmem()] * 6 + [hbm()] * 2 + [vmem()] * 2,
        (plan, *rest),
        scratch=[pltpu.VMEM((2 * BLK, D), bf16)] + seen_scratch(4),
    )


def run_own(plan, *rest):
    whole = shape((ROWS, D), bf16)
    total = shape((ROWS, D), f32)
    return call(
        own_kernel,
        [whole, whole, total, total],
        [smem()] + [vmem()] * 8,
        (plan, *rest),
        scratch=[pltpu.VMEM((PAIRS, BLK, ROWS), f32), pltpu.VMEM((2 * BLK, D), bf16)]
        + seen_scratch(2),
    )


def run_first_sum(far2, pick, *rest):
    whole = shape((ROWS, D), f32)
    return call(
        first_sum_kernel, [whole, whole], [vmem(), smem()] + [vmem()] * 2, (far2, pick, *rest)
    )


def run_second_sum(pick, *rest):
    whole = shape((ROWS, D), bf16)
    return call(second_sum_kernel, [whole, whole], [smem()] + [vmem()] * 6, (pick, *rest))


def sides(chip, cross):
    count = lax.axis_size("narrow")
    across = [(i, i + 1) for i in range(1, count - 1, 2)]
    return (
        lax.ppermute(chip, "narrow", [(i, i ^ 1) for i in range(count)]),
        lax.ppermute(cross, "narrow", across + [(b, a) for a, b in across]),
    )


def partner(value, distance):
    mask = 2**distance
    return lax.ppermute(value, "wide", [(s, s ^ mask) for s in range(lax.axis_size("wide"))])


def shift(value, axis, step):
    count = lax.axis_size(axis)
    pairs = [(s, s + step) for s in range(count) if 0 <= s + step < count]
    return lax.ppermute(value, axis, pairs)


def on_device(queries, key_rows, value_rows, upstream, pattern, expander_pick):
    wide_total = lax.axis_size("wide")
    narrow_total = lax.axis_size("narrow")
    wide_pos = lax.axis_index("wide")
    narrow_pos = lax.axis_index("narrow")
    top_bit = wide_total.bit_length() - 1

    even = narrow_pos & 1 == 0
    near_side = jnp.where(even, pattern[:, 6:8], pattern[:, 4:6])
    far_side = jnp.where(even, pattern[:, 4:6], pattern[:, 6:8])
    inner = (narrow_pos > 0) & (narrow_pos < narrow_total - 1)
    plan = jnp.concatenate(
        [
            pattern[:, 0:2],
            jnp.where(wide_pos > 0, pattern[:, 2:3], 0),
            jnp.where(wide_pos < wide_total - 1, pattern[:, 3:4], 0),
            near_side,
            jnp.where(inner, far_side, 0),
            pattern[:, 8:],
        ],
        axis=1,
    )

    far2_pair, whole = pack_first(expander_pick, key_rows, value_rows)
    chip, cross = sides(whole, whole)
    far2 = partner(far2_pair, top_bit - EXP)
    right_pair, left_pair, far0_pair, far1_pair = pack_rest(
        expander_pick, chip, cross, whole
    )
    far0 = partner(far0_pair, top_bit - 1)
    far1 = partner(far1_pair, top_bit - 2)
    left = shift(left_pair, "wide", 1)
    right = shift(right_pair, "wide", -1)
    stat, acc, upward_t = run_first(plan, queries, upstream, whole, chip, cross)
    stat, acc = run_far(far2, plan, queries, stat, acc)
    stat, out_t, query_t, far2_term, chip_term, cross_term = run_middle(
        far2, plan, queries, upstream, chip, cross, far0, far1, left, right, stat, acc, upward_t
    )
    far2_back = partner(far2_term, top_bit - EXP)
    back = sides(chip_term, cross_term)
    left_term, right_term, far0_term, far1_term, query_t = run_rest(
        plan, queries, upstream, left, right, far0, far1, *back, stat, query_t
    )
    attention, query_grad, key_near, value_near = run_own(
        plan, queries, upstream, whole, *back, stat, out_t, query_t
    )
    key_sum, value_sum = run_first_sum(far2_back, expander_pick, key_near, value_near)
    key_grad, value_grad = run_second_sum(
        expander_pick,
        key_sum,
        value_sum,
        partner(far0_term, top_bit - 1),
        partner(far1_term, top_bit - 2),
        shift(right_term, "wide", 1),
        shift(left_term, "wide", -1),
    )
    return (attention, query_grad, key_grad, value_grad)


def solution(mesh):
    placed = P(("wide", "narrow"), None)
    return jax.shard_map(
        on_device,
        mesh=mesh,
        in_specs=(placed,) * 6,
        out_specs=(placed,) * 4,
        check_vma=False,
    )
```

```python
import jax
import jax.numpy as jnp
from jax import lax
from jax.experimental import pallas as pl
from jax.experimental.pallas import tpu as pltpu
from jax.sharding import PartitionSpec as P

D = 768
HD = 64
BLK = 128
BW = 2
EXP = 3
ROWS = BW * BLK
MARK = 16
PAIRS = D // BLK
GROUP = 6
SCALE = HD ** (-0.5)
LOG2 = SCALE * 1.4426950408889634
HIDDEN = -1e30

VMEM_LIMIT = 24 * 1024 * 1024
NT = (((1,), (1,)), ((), ()))
NN = (((1,), (0,)), ((), ()))
f32 = jnp.float32
bf16 = jnp.bfloat16


def vmem():
    return pl.BlockSpec(memory_space=pltpu.VMEM)


def smem():
    return pl.BlockSpec(memory_space=pltpu.SMEM)


def dot(a, b, dims):
    return lax.dot_general(a, b, dims, preferred_element_type=f32)


def lanes(pair):
    return pl.ds(pl.multiple_of(pair * BLK, BLK), BLK)


def low_lane(shape):
    return lax.broadcasted_iota(jnp.int32, shape, 1) < HD


def low_row(shape):
    return lax.broadcasted_iota(jnp.int32, shape, 0) < HD


def stacked(tile):
    low = low_lane(tile.shape)
    zero = jnp.zeros_like(tile)
    return jnp.concatenate([jnp.where(low, tile, zero), jnp.where(low, zero, tile)], axis=0)


def stacked_t(tile):
    turned = tile.astype(f32).T
    low = low_row(turned.shape)
    zero = jnp.zeros_like(turned)
    return jnp.concatenate(
        [jnp.where(low, turned, zero), jnp.where(low, zero, turned)], axis=1
    ).astype(bf16)


def by_head(stat):
    return jnp.concatenate(
        [jnp.broadcast_to(stat[0:1], (BLK, ROWS)), jnp.broadcast_to(stat[1:2], (BLK, ROWS))], axis=0
    )


def by_feature(stat):
    return jnp.concatenate(
        [jnp.broadcast_to(stat[0:1], (HD, ROWS)), jnp.broadcast_to(stat[1:2], (HD, ROWS))], axis=0
    )


def seen_row(seen0, seen1):
    first = lax.broadcasted_iota(jnp.int32, (1, ROWS), 1) < BLK
    return jnp.where(first, seen0, seen1) > 0


def head_reduce(fn, tile):
    half = tile.shape[0] // 2
    return jnp.concatenate(
        [fn(tile[:half], axis=0, keepdims=True), fn(tile[half:], axis=0, keepdims=True)], axis=0
    )


def scores_t(key_tile, query_tile):
    return dot(stacked(key_tile), query_tile, NT)


def online(keys, values, queries, row, stat_ref, acc_ref, pairs):
    scores = [scores_t(k, q) for k, q in zip(keys, queries)]
    turned = [stacked_t(v) for v in values]
    probs, decays = [], []
    for pair, tile in zip(pairs, scores):
        old = stat_ref[pair, 0:2, :]
        new = jnp.where(row, jnp.maximum(old, head_reduce(jnp.max, tile) * LOG2), old)
        decay = jnp.exp2(old - new)
        weight = jnp.exp2(tile * LOG2 - by_head(jnp.where(row, new, -HIDDEN)))
        stat_ref[pair, 0:2, :] = new
        stat_ref[pair, 2:4, :] = stat_ref[pair, 2:4, :] * decay + head_reduce(jnp.sum, weight)
        probs.append(weight.astype(bf16))
        decays.append(decay)
    for i, pair in enumerate(pairs):
        acc_ref[pair] = acc_ref[pair] * by_feature(decays[i]) + dot(turned[i], probs[i], NN)


def own_head(product):
    return jnp.where(low_lane((BLK, BLK)), product[:BLK], product[BLK:])


def backward(keys, values, queries, upwards, row, stats):
    scores = [scores_t(k, q) for k, q in zip(keys, queries)]
    products = [dot(stacked(v), u, NT) for v, u in zip(values, upwards)]
    weights, grads = [], []
    for tile, product, stat in zip(scores, products, stats):
        weight = jnp.exp2(tile * LOG2 - by_head(jnp.where(row, stat[0:2], -HIDDEN)))
        weights.append(weight.astype(bf16))
        grads.append((weight * (product - by_head(stat[2:4]))).astype(bf16))
    value_terms = [own_head(dot(w, u, NN)).astype(bf16) for w, u in zip(weights, upwards)]
    key_terms = [(own_head(dot(g, q, NN)) * SCALE).astype(bf16) for g, q in zip(grads, queries)]
    query_ts = [dot(stacked_t(k), g, NN) for k, g in zip(keys, grads)]
    return key_terms, value_terms, query_ts


def groups():
    return [range(first, first + GROUP) for first in range(0, PAIRS, GROUP)]


def own_slots(whole):
    return [(b, whole, b * BLK, whole, ROWS + b * BLK) for b in range(BW)]


def side_slots(chip, cross):
    return [
        (4 + BW * i + b, ref, b * BLK, ref, ROWS + b * BLK)
        for i, ref in enumerate((chip, cross))
        for b in range(BW)
    ]


def pair_slots(columns, *refs):
    return [(j, ref, 0, ref, BLK) for j, ref in zip(columns, refs)]


def rest_slots(left, right, far0, far1):
    return pair_slots((2, 3, 8, 9), left, right, far0, far1)


def rows_at(start):
    return pl.ds(start if isinstance(start, int) else pl.multiple_of(start, BLK), BLK)


def feature(pair):
    return slice(pair * BLK, (pair + 1) * BLK)


def load_seen(seen, slots, held, place):
    count = jnp.int32(0)
    for j, k_ref, k_row, v_ref, v_row in slots:
        used = seen[0, j] + seen[1, j] > 0
        at = count

        @pl.when(used)
        def _():
            place[at] = j
            held[at, 0:BLK] = k_ref[rows_at(k_row)]
            held[at, BLK : 2 * BLK] = v_ref[rows_at(v_row)]

        count = count + used.astype(jnp.int32)
    return count


def forward_over(slots, seen, query, stat, acc, held, place):
    count = load_seen(seen, slots, held, place)

    def step(at, carry):
        j = place[at]
        row = seen_row(seen[0, j], seen[1, j])
        for pairs in groups():
            online(
                [held[at, 0:BLK, feature(p)] for p in pairs],
                [held[at, BLK : 2 * BLK, feature(p)] for p in pairs],
                [query[:, feature(p)] for p in pairs],
                row,
                stat,
                acc,
                pairs,
            )
        return carry

    lax.fori_loop(0, count, step, 0)


def first_kernel(seen, query, upward, whole, chip, cross, stat, acc, upward_t, held, place):
    for pair in range(PAIRS):
        stat[pair, 0:2, :] = jnp.full((2, ROWS), HIDDEN, f32)
        stat[pair, 2:4, :] = jnp.zeros((2, ROWS), f32)
        acc[pair] = jnp.zeros((BLK, ROWS), f32)
        upward_t[pair] = upward[:, feature(pair)].astype(f32).T
    forward_over(
        own_slots(whole) + side_slots(chip, cross), seen, query, stat, acc, held, place
    )


def far_kernel(far2, seen, query, stat_in, acc_in, stat, acc, wanted, held, place):
    partner_sees = jnp.max(far2[2 * BLK :].astype(f32)) > 0
    wanted[0, 0] = ((seen[0, 10] + seen[1, 10] > 0) | partner_sees).astype(jnp.int32)
    stat[...] = stat_in[...]
    acc[...] = acc_in[...]
    forward_over(pair_slots((10,), far2), seen, query, stat, acc, held, place)


def clear_unseen(slots, seen):
    for j, k_ref, k_row, v_ref, v_row in slots:

        @pl.when(seen[0, j] + seen[1, j] == 0)
        def _():
            k_ref[k_row : k_row + BLK] = jnp.zeros((BLK, D), bf16)
            v_ref[v_row : v_row + BLK] = jnp.zeros((BLK, D), bf16)


def backward_over(sources, seen, query, upward, stat, query_t, held, place, terms, store):
    count = load_seen(seen, sources, held, place)

    def step(at, carry):
        j = place[at]
        row = seen_row(seen[0, j], seen[1, j])
        for pairs in groups():
            key_terms, value_terms, grads = backward(
                [held[at, 0:BLK, feature(p)] for p in pairs],
                [held[at, BLK : 2 * BLK, feature(p)] for p in pairs],
                [query[:, feature(p)] for p in pairs],
                [upward[:, feature(p)] for p in pairs],
                row,
                [stat[p] for p in pairs],
            )
            for i, pair in enumerate(pairs):
                terms[0:BLK, feature(pair)] = key_terms[i]
                terms[BLK : 2 * BLK, feature(pair)] = value_terms[i]
                query_t[pair] = query_t[pair] + grads[i]
        store(j)
        return carry

    lax.fori_loop(0, count, step, 0)


def store_terms(slots, terms, j):
    for slot, k_ref, k_row, v_ref, v_row in slots:

        @pl.when(j == slot)
        def _():
            k_ref[k_row : k_row + BLK] = terms[0:BLK]
            v_ref[v_row : v_row + BLK] = terms[BLK : 2 * BLK]


def middle_kernel(
    far2,
    seen,
    query,
    upward,
    chip,
    cross,
    far0,
    far1,
    left,
    right,
    stat_in,
    acc_in,
    upward_t,
    stat,
    out_t,
    query_t,
    far2_term,
    chip_term,
    cross_term,
    acc,
    terms,
    held,
    place,
):
    stat[...] = stat_in[...]
    acc[...] = acc_in[...]
    forward_over(rest_slots(left, right, far0, far1), seen, query, stat, acc, held, place)

    for pair in range(PAIRS):
        total = stat[pair, 2:4, :]
        attended = (acc[pair] * by_feature(1.0 / total)).astype(bf16)
        out_t[pair] = attended
        stat[pair, 0:2, :] = stat[pair, 0:2, :] + jnp.log2(total)
        stat[pair, 2:4, :] = head_reduce(jnp.sum, upward_t[pair] * attended.astype(f32))

    query_t[...] = jnp.zeros_like(query_t)
    targets = pair_slots((10,), far2_term) + side_slots(chip_term, cross_term)
    clear_unseen(targets, seen)
    backward_over(
        pair_slots((10,), far2) + side_slots(chip, cross),
        seen,
        query,
        upward,
        stat,
        query_t,
        held,
        place,
        terms,
        lambda j: store_terms(targets, terms, j),
    )


def rest_kernel(
    seen,
    query,
    upward,
    left,
    right,
    far0,
    far1,
    chip_back,
    cross_back,
    stat,
    query_t_in,
    left_term,
    right_term,
    far0_term,
    far1_term,
    query_t,
    terms,
    held,
    place,
):
    query_t[...] = query_t_in[...]
    targets = rest_slots(left_term, right_term, far0_term, far1_term)
    clear_unseen(targets, seen)
    backward_over(
        rest_slots(left, right, far0, far1),
        seen,
        query,
        upward,
        stat,
        query_t,
        held,
        place,
        terms,
        lambda j: store_terms(targets, terms, j),
    )


def own_kernel(
    seen,
    query,
    upward,
    whole,
    chip_back,
    cross_back,
    stat,
    out_t,
    query_t_in,
    attention,
    query_grad,
    key_sum,
    value_sum,
    query_t,
    terms,
    held,
    place,
):
    query_t[...] = query_t_in[...]
    for pair in range(PAIRS):
        attention[:, feature(pair)] = out_t[pair].astype(f32).T.astype(bf16)

    def store(j):
        for b in range(BW):

            @pl.when(j == b)
            def _():
                for half, out in enumerate((key_sum, value_sum)):
                    side = slice(half * ROWS + b * BLK, half * ROWS + (b + 1) * BLK)
                    out[b * BLK : (b + 1) * BLK] = (
                        terms[half * BLK : (half + 1) * BLK].astype(f32)
                        + chip_back[side].astype(f32)
                        + cross_back[side].astype(f32)
                    )

    backward_over(
        own_slots(whole), seen, query, upward, stat, query_t, held, place, terms, store
    )
    for pair in range(PAIRS):
        query_grad[:, feature(pair)] = (query_t[pair] * SCALE).T.astype(bf16)


def first_sum_kernel(far2, pick, key_near, value_near, key_sum, value_sum):
    for half, (near, out) in enumerate(((key_near, key_sum), (value_near, value_sum))):
        far_part = far2[half * BLK : (half + 1) * BLK].astype(f32)
        for b in range(BW):
            rows = slice(b * BLK, (b + 1) * BLK)
            out[rows] = near[rows] + jnp.where(pick[0, 2] == b, far_part, 0.0)


def second_sum_kernel(pick, key_sum, value_sum, far0, far1, low_block, high_block, key_grad, value_grad):
    for half, (near, out) in enumerate(((key_sum, key_grad), (value_sum, value_grad))):
        part = slice(half * BLK, (half + 1) * BLK)
        for b in range(BW):
            rows = slice(b * BLK, (b + 1) * BLK)
            total = near[rows]
            if b == 0:
                total = total + low_block[part].astype(f32)
            if b == BW - 1:
                total = total + high_block[part].astype(f32)
            for slot, far in enumerate((far0, far1)):
                total = total + jnp.where(pick[0, slot] == b, far[part].astype(f32), 0.0)
            out[rows] = total.astype(bf16)


def call(kernel, shapes, specs, args, scratch=(), outs=None, cost=None):
    return pl.pallas_call(
        kernel,
        out_shape=shapes,
        in_specs=specs,
        out_specs=outs if outs is not None else jax.tree.map(lambda _: vmem(), shapes),
        scratch_shapes=list(scratch),
        compiler_params=pltpu.CompilerParams(vmem_limit_bytes=VMEM_LIMIT),
        cost_estimate=cost,
    )(*args)


def shape(dims, dtype):
    return jax.ShapeDtypeStruct(dims, dtype)


def hbm():
    return pl.BlockSpec(memory_space=pl.ANY)


STATE = [shape((PAIRS, 8, ROWS), f32), shape((PAIRS, BLK, ROWS), f32)]
RIM = shape((2 * BLK, D), bf16)
SIDE = shape((2 * ROWS, D), bf16)


def block_of(whole, start, out):
    for half in range(2):
        rows = pl.ds(pl.multiple_of(half * ROWS + start, BLK), BLK)
        out[half * BLK : (half + 1) * BLK] = whole[rows]


def pack_first_kernel(pick, pattern, key, value, far2, whole):
    whole[0:ROWS] = key[...]
    whole[ROWS : 2 * ROWS] = value[...]
    block_of(whole, pick[0, 2] * BLK, far2)
    sees = (pattern[0, 10] + pattern[1, 10] > 0).astype(f32)
    far2[2 * BLK :] = jnp.full((MARK, D), sees, f32).astype(bf16)


def pack_rest_kernel(pick, chip, cross, whole, right, left, far0, far1):
    block_of(whole, 0, right)
    block_of(whole, ROWS - BLK, left)
    block_of(whole, pick[0, 0] * BLK, far0)
    block_of(whole, pick[0, 1] * BLK, far1)


def pack_first(pick, pattern, key, value):
    return call(
        pack_first_kernel,
        [shape((2 * BLK + MARK, D), bf16), SIDE],
        [smem(), smem(), vmem(), vmem()],
        (pick, pattern, key, value),
    )


def pack_rest(pick, chip, cross, whole):
    return call(
        pack_rest_kernel, [RIM] * 4, [smem(), hbm(), hbm(), vmem()], (pick, chip, cross, whole)
    )


def seen_scratch(slots):
    return [pltpu.VMEM((slots, 2 * BLK, D), bf16), pltpu.SMEM((16,), jnp.int32)]


def run_first(plan, *rest):
    return call(
        first_kernel,
        STATE + [shape((PAIRS, BLK, ROWS), f32)],
        [smem()] + [vmem()] * 5,
        (plan, *rest),
        scratch=seen_scratch(6),
    )


def run_far(far2, plan, queries, stat, acc):
    return call(
        far_kernel,
        STATE + [shape((1, 1), jnp.int32)],
        [vmem(), smem()] + [vmem()] * 3,
        (far2, plan, queries, stat, acc),
        outs=[vmem(), vmem(), smem()],
        scratch=seen_scratch(1),
    )


def run_middle(far2, plan, *rest):
    return call(
        middle_kernel,
        [STATE[0], shape((PAIRS, BLK, ROWS), bf16), STATE[1], RIM, SIDE, SIDE],
        [vmem(), smem()] + [vmem()] * 11,
        (far2, plan, *rest),
        scratch=[pltpu.VMEM((PAIRS, BLK, ROWS), f32), pltpu.VMEM((2 * BLK, D), bf16)]
        + seen_scratch(5),
    )


def run_rest(plan, *rest):
    return call(
        rest_kernel,
        [RIM] * 4 + [STATE[1]],
        [smem()] + [vmem()] * 6 + [hbm()] * 2 + [vmem()] * 2,
        (plan, *rest),
        scratch=[pltpu.VMEM((2 * BLK, D), bf16)] + seen_scratch(4),
    )


def run_own(plan, *rest):
    whole = shape((ROWS, D), bf16)
    total = shape((ROWS, D), f32)
    return call(
        own_kernel,
        [whole, whole, total, total],
        [smem()] + [vmem()] * 8,
        (plan, *rest),
        scratch=[pltpu.VMEM((PAIRS, BLK, ROWS), f32), pltpu.VMEM((2 * BLK, D), bf16)]
        + seen_scratch(2),
    )


def run_first_sum(far2, pick, *rest):
    whole = shape((ROWS, D), f32)
    return call(
        first_sum_kernel, [whole, whole], [vmem(), smem()] + [vmem()] * 2, (far2, pick, *rest)
    )


def run_second_sum(pick, *rest):
    whole = shape((ROWS, D), bf16)
    return call(second_sum_kernel, [whole, whole], [smem()] + [vmem()] * 6, (pick, *rest))


def sides(chip, cross):
    count = lax.axis_size("narrow")
    across = [(i, i + 1) for i in range(1, count - 1, 2)]
    return (
        lax.ppermute(chip, "narrow", [(i, i ^ 1) for i in range(count)]),
        lax.ppermute(cross, "narrow", across + [(b, a) for a, b in across]),
    )


def partner(value, distance):
    mask = 2**distance
    return lax.ppermute(value, "wide", [(s, s ^ mask) for s in range(lax.axis_size("wide"))])


def shift(value, axis, step):
    count = lax.axis_size(axis)
    pairs = [(s, s + step) for s in range(count) if 0 <= s + step < count]
    return lax.ppermute(value, axis, pairs)


def on_device(queries, key_rows, value_rows, upstream, pattern, expander_pick):
    wide_total = lax.axis_size("wide")
    narrow_total = lax.axis_size("narrow")
    wide_pos = lax.axis_index("wide")
    narrow_pos = lax.axis_index("narrow")
    top_bit = wide_total.bit_length() - 1

    even = narrow_pos & 1 == 0
    near_side = jnp.where(even, pattern[:, 6:8], pattern[:, 4:6])
    far_side = jnp.where(even, pattern[:, 4:6], pattern[:, 6:8])
    inner = (narrow_pos > 0) & (narrow_pos < narrow_total - 1)
    plan = jnp.concatenate(
        [
            pattern[:, 0:2],
            jnp.where(wide_pos > 0, pattern[:, 2:3], 0),
            jnp.where(wide_pos < wide_total - 1, pattern[:, 3:4], 0),
            near_side,
            jnp.where(inner, far_side, 0),
            pattern[:, 8:],
        ],
        axis=1,
    )

    far2_pair, whole = pack_first(expander_pick, pattern, key_rows, value_rows)
    chip, cross = sides(whole, whole)
    far2 = partner(far2_pair, top_bit - EXP)
    right_pair, left_pair, far0_pair, far1_pair = pack_rest(
        expander_pick, chip, cross, whole
    )
    far0 = partner(far0_pair, top_bit - 1)
    far1 = partner(far1_pair, top_bit - 2)
    left = shift(left_pair, "wide", 1)
    right = shift(right_pair, "wide", -1)
    stat, acc, upward_t = run_first(plan, queries, upstream, whole, chip, cross)
    stat, acc, wanted = run_far(far2, plan, queries, stat, acc)
    stat, out_t, query_t, far2_term, chip_term, cross_term = run_middle(
        far2, plan, queries, upstream, chip, cross, far0, far1, left, right, stat, acc, upward_t
    )
    back = sides(chip_term, cross_term)
    left_term, right_term, far0_term, far1_term, query_t = run_rest(
        plan, queries, upstream, left, right, far0, far1, *back, stat, query_t
    )

    def own_and_exchange(term, *args):
        return partner(term, top_bit - EXP), run_own(*args)

    def own_alone(term, *args):
        return term, run_own(*args)

    far2_back, (attention, query_grad, key_near, value_near) = lax.cond(
        wanted[0, 0] > 0,
        own_and_exchange,
        own_alone,
        far2_term,
        plan,
        queries,
        upstream,
        whole,
        *back,
        stat,
        out_t,
        query_t,
    )
    key_sum, value_sum = run_first_sum(far2_back, expander_pick, key_near, value_near)
    key_grad, value_grad = run_second_sum(
        expander_pick,
        key_sum,
        value_sum,
        partner(far0_term, top_bit - 1),
        partner(far1_term, top_bit - 2),
        shift(right_term, "wide", 1),
        shift(left_term, "wide", -1),
    )
    return (attention, query_grad, key_grad, value_grad)


def solution(mesh):
    placed = P(("wide", "narrow"), None)
    return jax.shard_map(
        on_device,
        mesh=mesh,
        in_specs=(placed,) * 6,
        out_specs=(placed,) * 4,
        check_vma=False,
    )
```

```python
import jax
import jax.numpy as jnp
from jax import lax
from jax.experimental import pallas as pl
from jax.experimental.pallas import tpu as pltpu
from jax.sharding import PartitionSpec as P

D = 768
HD = 64
BLK = 128
BW = 2
EXP = 3
ROWS = BW * BLK
MARK = 16
PAIRS = D // BLK
GROUP = 6
SCALE = HD ** (-0.5)
LOG2 = SCALE * 1.4426950408889634
HIDDEN = -1e30

VMEM_LIMIT = 24 * 1024 * 1024
NT = (((1,), (1,)), ((), ()))
NN = (((1,), (0,)), ((), ()))
f32 = jnp.float32
bf16 = jnp.bfloat16


def vmem():
    return pl.BlockSpec(memory_space=pltpu.VMEM)


def smem():
    return pl.BlockSpec(memory_space=pltpu.SMEM)


def dot(a, b, dims):
    return lax.dot_general(a, b, dims, preferred_element_type=f32)


def lanes(pair):
    return pl.ds(pl.multiple_of(pair * BLK, BLK), BLK)


def low_lane(shape):
    return lax.broadcasted_iota(jnp.int32, shape, 1) < HD


def low_row(shape):
    return lax.broadcasted_iota(jnp.int32, shape, 0) < HD


def stacked(tile):
    low = low_lane(tile.shape)
    zero = jnp.zeros_like(tile)
    return jnp.concatenate([jnp.where(low, tile, zero), jnp.where(low, zero, tile)], axis=0)


def stacked_t(tile):
    turned = tile.astype(f32).T
    low = low_row(turned.shape)
    zero = jnp.zeros_like(turned)
    return jnp.concatenate(
        [jnp.where(low, turned, zero), jnp.where(low, zero, turned)], axis=1
    ).astype(bf16)


def by_head(stat):
    return jnp.concatenate(
        [jnp.broadcast_to(stat[0:1], (BLK, ROWS)), jnp.broadcast_to(stat[1:2], (BLK, ROWS))], axis=0
    )


def by_feature(stat):
    return jnp.concatenate(
        [jnp.broadcast_to(stat[0:1], (HD, ROWS)), jnp.broadcast_to(stat[1:2], (HD, ROWS))], axis=0
    )


def seen_row(seen0, seen1):
    first = lax.broadcasted_iota(jnp.int32, (1, ROWS), 1) < BLK
    return jnp.where(first, seen0, seen1) > 0


def head_reduce(fn, tile):
    half = tile.shape[0] // 2
    return jnp.concatenate(
        [fn(tile[:half], axis=0, keepdims=True), fn(tile[half:], axis=0, keepdims=True)], axis=0
    )


def scores_t(key_tile, query_tile):
    return dot(stacked(key_tile), query_tile, NT)


def online(keys, values, queries, row, stat_ref, acc_ref, pairs):
    scores = [scores_t(k, q) for k, q in zip(keys, queries)]
    turned = [stacked_t(v) for v in values]
    probs, decays = [], []
    for pair, tile in zip(pairs, scores):
        old = stat_ref[pair, 0:2, :]
        new = jnp.where(row, jnp.maximum(old, head_reduce(jnp.max, tile) * LOG2), old)
        decay = jnp.exp2(old - new)
        weight = jnp.exp2(tile * LOG2 - by_head(jnp.where(row, new, -HIDDEN)))
        stat_ref[pair, 0:2, :] = new
        stat_ref[pair, 2:4, :] = stat_ref[pair, 2:4, :] * decay + head_reduce(jnp.sum, weight)
        probs.append(weight.astype(bf16))
        decays.append(decay)
    for i, pair in enumerate(pairs):
        acc_ref[pair] = acc_ref[pair] * by_feature(decays[i]) + dot(turned[i], probs[i], NN)


def own_head(product):
    return jnp.where(low_lane((BLK, BLK)), product[:BLK], product[BLK:])


def backward(keys, values, queries, upwards, row, stats):
    scores = [scores_t(k, q) for k, q in zip(keys, queries)]
    products = [dot(stacked(v), u, NT) for v, u in zip(values, upwards)]
    weights, grads = [], []
    for tile, product, stat in zip(scores, products, stats):
        weight = jnp.exp2(tile * LOG2 - by_head(jnp.where(row, stat[0:2], -HIDDEN)))
        weights.append(weight.astype(bf16))
        grads.append((weight * (product - by_head(stat[2:4]))).astype(bf16))
    value_terms = [own_head(dot(w, u, NN)).astype(bf16) for w, u in zip(weights, upwards)]
    key_terms = [(own_head(dot(g, q, NN)) * SCALE).astype(bf16) for g, q in zip(grads, queries)]
    query_ts = [dot(stacked_t(k), g, NN) for k, g in zip(keys, grads)]
    return key_terms, value_terms, query_ts


def groups():
    return [range(first, first + GROUP) for first in range(0, PAIRS, GROUP)]


def own_slots(whole):
    return [(b, whole, b * BLK, whole, ROWS + b * BLK) for b in range(BW)]


def side_slots(chip, cross):
    return [
        (4 + BW * i + b, ref, b * BLK, ref, ROWS + b * BLK)
        for i, ref in enumerate((chip, cross))
        for b in range(BW)
    ]


def pair_slots(columns, *refs):
    return [(j, ref, 0, ref, BLK) for j, ref in zip(columns, refs)]


def rest_slots(left, right, far0, far1):
    return pair_slots((2, 3, 8, 9), left, right, far0, far1)


def rows_at(start):
    return pl.ds(start if isinstance(start, int) else pl.multiple_of(start, BLK), BLK)


def feature(pair):
    return slice(pair * BLK, (pair + 1) * BLK)


def load_seen(seen, slots, held, place):
    count = jnp.int32(0)
    for j, k_ref, k_row, v_ref, v_row in slots:
        used = seen[0, j] + seen[1, j] > 0
        at = count

        @pl.when(used)
        def _():
            place[at] = j
            held[at, 0:BLK] = k_ref[rows_at(k_row)]
            held[at, BLK : 2 * BLK] = v_ref[rows_at(v_row)]

        count = count + used.astype(jnp.int32)
    return count


def forward_over(slots, seen, query, stat, acc, held, place):
    count = load_seen(seen, slots, held, place)

    def step(at, carry):
        j = place[at]
        row = seen_row(seen[0, j], seen[1, j])
        for pairs in groups():
            online(
                [held[at, 0:BLK, feature(p)] for p in pairs],
                [held[at, BLK : 2 * BLK, feature(p)] for p in pairs],
                [query[:, feature(p)] for p in pairs],
                row,
                stat,
                acc,
                pairs,
            )
        return carry

    lax.fori_loop(0, count, step, 0)


def first_kernel(seen, query, upward, whole, chip, cross, stat, acc, upward_t, held, place):
    for pair in range(PAIRS):
        stat[pair, 0:2, :] = jnp.full((2, ROWS), HIDDEN, f32)
        stat[pair, 2:4, :] = jnp.zeros((2, ROWS), f32)
        acc[pair] = jnp.zeros((BLK, ROWS), f32)
        upward_t[pair] = upward[:, feature(pair)].astype(f32).T
    forward_over(
        own_slots(whole) + side_slots(chip, cross), seen, query, stat, acc, held, place
    )


def far_kernel(far2, seen, query, stat_in, acc_in, stat, acc, wanted, held, place):
    partner_sees = jnp.max(far2[2 * BLK :].astype(f32)) > 0
    wanted[0, 0] = ((seen[0, 10] + seen[1, 10] > 0) | partner_sees).astype(jnp.int32)
    stat[...] = stat_in[...]
    acc[...] = acc_in[...]
    forward_over(pair_slots((10,), far2), seen, query, stat, acc, held, place)


def clear_unseen(slots, seen):
    for j, k_ref, k_row, v_ref, v_row in slots:

        @pl.when(seen[0, j] + seen[1, j] == 0)
        def _():
            k_ref[k_row : k_row + BLK] = jnp.zeros((BLK, D), bf16)
            v_ref[v_row : v_row + BLK] = jnp.zeros((BLK, D), bf16)


def backward_over(sources, seen, query, upward, stat, query_t, held, place, terms, store):
    count = load_seen(seen, sources, held, place)

    def step(at, carry):
        j = place[at]
        row = seen_row(seen[0, j], seen[1, j])
        for pairs in groups():
            key_terms, value_terms, grads = backward(
                [held[at, 0:BLK, feature(p)] for p in pairs],
                [held[at, BLK : 2 * BLK, feature(p)] for p in pairs],
                [query[:, feature(p)] for p in pairs],
                [upward[:, feature(p)] for p in pairs],
                row,
                [stat[p] for p in pairs],
            )
            for i, pair in enumerate(pairs):
                terms[0:BLK, feature(pair)] = key_terms[i]
                terms[BLK : 2 * BLK, feature(pair)] = value_terms[i]
                query_t[pair] = query_t[pair] + grads[i]
        store(j)
        return carry

    lax.fori_loop(0, count, step, 0)


def store_terms(slots, terms, j):
    for slot, k_ref, k_row, v_ref, v_row in slots:

        @pl.when(j == slot)
        def _():
            k_ref[k_row : k_row + BLK] = terms[0:BLK]
            v_ref[v_row : v_row + BLK] = terms[BLK : 2 * BLK]


def middle_kernel(
    far2,
    seen,
    query,
    upward,
    chip,
    cross,
    far0,
    far1,
    left,
    right,
    stat_in,
    acc_in,
    upward_t,
    stat,
    out_t,
    query_t,
    far2_term,
    chip_term,
    cross_term,
    acc,
    terms,
    held,
    place,
):
    stat[...] = stat_in[...]
    acc[...] = acc_in[...]
    forward_over(rest_slots(left, right, far0, far1), seen, query, stat, acc, held, place)

    for pair in range(PAIRS):
        total = stat[pair, 2:4, :]
        attended = (acc[pair] * by_feature(1.0 / total)).astype(bf16)
        out_t[pair] = attended
        stat[pair, 0:2, :] = stat[pair, 0:2, :] + jnp.log2(total)
        stat[pair, 2:4, :] = head_reduce(jnp.sum, upward_t[pair] * attended.astype(f32))

    query_t[...] = jnp.zeros_like(query_t)
    targets = pair_slots((10,), far2_term) + side_slots(chip_term, cross_term)
    clear_unseen(targets, seen)
    backward_over(
        pair_slots((10,), far2) + side_slots(chip, cross),
        seen,
        query,
        upward,
        stat,
        query_t,
        held,
        place,
        terms,
        lambda j: store_terms(targets, terms, j),
    )


def rest_kernel(
    seen,
    query,
    upward,
    left,
    right,
    far0,
    far1,
    stat,
    query_t_in,
    left_term,
    right_term,
    far0_term,
    far1_term,
    query_t,
    terms,
    held,
    place,
):
    query_t[...] = query_t_in[...]
    targets = rest_slots(left_term, right_term, far0_term, far1_term)
    clear_unseen(targets, seen)
    backward_over(
        rest_slots(left, right, far0, far1),
        seen,
        query,
        upward,
        stat,
        query_t,
        held,
        place,
        terms,
        lambda j: store_terms(targets, terms, j),
    )


def own_kernel(
    seen,
    query,
    upward,
    whole,
    chip_back,
    cross_back,
    stat,
    out_t,
    query_t_in,
    attention,
    query_grad,
    key_sum,
    value_sum,
    query_t,
    terms,
    held,
    place,
):
    query_t[...] = query_t_in[...]
    for pair in range(PAIRS):
        attention[:, feature(pair)] = out_t[pair].astype(f32).T.astype(bf16)

    def store(j):
        for b in range(BW):

            @pl.when(j == b)
            def _():
                for half, out in enumerate((key_sum, value_sum)):
                    side = slice(half * ROWS + b * BLK, half * ROWS + (b + 1) * BLK)
                    out[b * BLK : (b + 1) * BLK] = (
                        terms[half * BLK : (half + 1) * BLK].astype(f32)
                        + chip_back[side].astype(f32)
                        + cross_back[side].astype(f32)
                    )

    backward_over(
        own_slots(whole), seen, query, upward, stat, query_t, held, place, terms, store
    )
    for pair in range(PAIRS):
        query_grad[:, feature(pair)] = (query_t[pair] * SCALE).T.astype(bf16)


def first_sum_kernel(far2, pick, key_near, value_near, key_sum, value_sum):
    for half, (near, out) in enumerate(((key_near, key_sum), (value_near, value_sum))):
        far_part = far2[half * BLK : (half + 1) * BLK].astype(f32)
        for b in range(BW):
            rows = slice(b * BLK, (b + 1) * BLK)
            out[rows] = near[rows] + jnp.where(pick[0, 2] == b, far_part, 0.0)


def second_sum_kernel(pick, key_sum, value_sum, far0, far1, low_block, high_block, key_grad, value_grad):
    for half, (near, out) in enumerate(((key_sum, key_grad), (value_sum, value_grad))):
        part = slice(half * BLK, (half + 1) * BLK)
        for b in range(BW):
            rows = slice(b * BLK, (b + 1) * BLK)
            total = near[rows]
            if b == 0:
                total = total + low_block[part].astype(f32)
            if b == BW - 1:
                total = total + high_block[part].astype(f32)
            for slot, far in enumerate((far0, far1)):
                total = total + jnp.where(pick[0, slot] == b, far[part].astype(f32), 0.0)
            out[rows] = total.astype(bf16)


def call(kernel, shapes, specs, args, scratch=(), outs=None, cost=None):
    return pl.pallas_call(
        kernel,
        out_shape=shapes,
        in_specs=specs,
        out_specs=outs if outs is not None else jax.tree.map(lambda _: vmem(), shapes),
        scratch_shapes=list(scratch),
        compiler_params=pltpu.CompilerParams(vmem_limit_bytes=VMEM_LIMIT),
        cost_estimate=cost,
    )(*args)


def shape(dims, dtype):
    return jax.ShapeDtypeStruct(dims, dtype)


def hbm():
    return pl.BlockSpec(memory_space=pl.ANY)


STATE = [shape((PAIRS, 8, ROWS), f32), shape((PAIRS, BLK, ROWS), f32)]
RIM = shape((2 * BLK, D), bf16)
SIDE = shape((2 * ROWS, D), bf16)


def block_of(whole, start, out):
    for half in range(2):
        rows = pl.ds(pl.multiple_of(half * ROWS + start, BLK), BLK)
        out[half * BLK : (half + 1) * BLK] = whole[rows]


def pack_first_kernel(pick, pattern, key, value, far2, whole):
    whole[0:ROWS] = key[...]
    whole[ROWS : 2 * ROWS] = value[...]
    block_of(whole, pick[0, 2] * BLK, far2)
    sees = (pattern[0, 10] + pattern[1, 10] > 0).astype(f32)
    far2[2 * BLK :] = jnp.full((MARK, D), sees, f32).astype(bf16)


def pack_rest_kernel(pick, chip, cross, whole, right, left, far0, far1):
    block_of(whole, 0, right)
    block_of(whole, ROWS - BLK, left)
    block_of(whole, pick[0, 0] * BLK, far0)
    block_of(whole, pick[0, 1] * BLK, far1)


def pack_first(pick, pattern, key, value):
    return call(
        pack_first_kernel,
        [shape((2 * BLK + MARK, D), bf16), SIDE],
        [smem(), smem(), vmem(), vmem()],
        (pick, pattern, key, value),
    )


def pack_rest(pick, chip, cross, whole):
    return call(
        pack_rest_kernel, [RIM] * 4, [smem(), hbm(), hbm(), vmem()], (pick, chip, cross, whole)
    )


def seen_scratch(slots):
    return [pltpu.VMEM((slots, 2 * BLK, D), bf16), pltpu.SMEM((16,), jnp.int32)]


def run_first(plan, *rest):
    return call(
        first_kernel,
        STATE + [shape((PAIRS, BLK, ROWS), f32)],
        [smem()] + [vmem()] * 5,
        (plan, *rest),
        scratch=seen_scratch(6),
    )


def run_far(far2, plan, queries, stat, acc):
    return call(
        far_kernel,
        STATE + [shape((1, 1), jnp.int32)],
        [vmem(), smem()] + [vmem()] * 3,
        (far2, plan, queries, stat, acc),
        outs=[vmem(), vmem(), smem()],
        scratch=seen_scratch(1),
    )


def run_middle(far2, plan, *rest):
    return call(
        middle_kernel,
        [STATE[0], shape((PAIRS, BLK, ROWS), bf16), STATE[1], RIM, SIDE, SIDE],
        [vmem(), smem()] + [vmem()] * 11,
        (far2, plan, *rest),
        scratch=[pltpu.VMEM((PAIRS, BLK, ROWS), f32), pltpu.VMEM((2 * BLK, D), bf16)]
        + seen_scratch(5),
    )


def run_rest(plan, *rest):
    return call(
        rest_kernel,
        [RIM] * 4 + [STATE[1]],
        [smem()] + [vmem()] * 8,
        (plan, *rest),
        scratch=[pltpu.VMEM((2 * BLK, D), bf16)] + seen_scratch(4),
    )


def run_own(plan, *rest):
    whole = shape((ROWS, D), bf16)
    total = shape((ROWS, D), f32)
    return call(
        own_kernel,
        [whole, whole, total, total],
        [smem()] + [vmem()] * 8,
        (plan, *rest),
        scratch=[pltpu.VMEM((PAIRS, BLK, ROWS), f32), pltpu.VMEM((2 * BLK, D), bf16)]
        + seen_scratch(2),
    )


def run_first_sum(far2, pick, *rest):
    whole = shape((ROWS, D), f32)
    return call(
        first_sum_kernel, [whole, whole], [vmem(), smem()] + [vmem()] * 2, (far2, pick, *rest)
    )


def run_second_sum(pick, *rest):
    whole = shape((ROWS, D), bf16)
    return call(second_sum_kernel, [whole, whole], [smem()] + [vmem()] * 6, (pick, *rest))


def sides(chip, cross):
    count = lax.axis_size("narrow")
    across = [(i, i + 1) for i in range(1, count - 1, 2)]
    return (
        lax.ppermute(chip, "narrow", [(i, i ^ 1) for i in range(count)]),
        lax.ppermute(cross, "narrow", across + [(b, a) for a, b in across]),
    )


def partner(value, distance):
    mask = 2**distance
    return lax.ppermute(value, "wide", [(s, s ^ mask) for s in range(lax.axis_size("wide"))])


def shift(value, axis, step):
    count = lax.axis_size(axis)
    pairs = [(s, s + step) for s in range(count) if 0 <= s + step < count]
    return lax.ppermute(value, axis, pairs)


def on_device(queries, key_rows, value_rows, upstream, pattern, expander_pick):
    wide_total = lax.axis_size("wide")
    narrow_total = lax.axis_size("narrow")
    wide_pos = lax.axis_index("wide")
    narrow_pos = lax.axis_index("narrow")
    top_bit = wide_total.bit_length() - 1

    even = narrow_pos & 1 == 0
    near_side = jnp.where(even, pattern[:, 6:8], pattern[:, 4:6])
    far_side = jnp.where(even, pattern[:, 4:6], pattern[:, 6:8])
    inner = (narrow_pos > 0) & (narrow_pos < narrow_total - 1)
    plan = jnp.concatenate(
        [
            pattern[:, 0:2],
            jnp.where(wide_pos > 0, pattern[:, 2:3], 0),
            jnp.where(wide_pos < wide_total - 1, pattern[:, 3:4], 0),
            near_side,
            jnp.where(inner, far_side, 0),
            pattern[:, 8:],
        ],
        axis=1,
    )

    far2_pair, whole = pack_first(expander_pick, pattern, key_rows, value_rows)
    chip, cross = sides(whole, whole)
    far2 = partner(far2_pair, top_bit - EXP)
    right_pair, left_pair, far0_pair, far1_pair = pack_rest(
        expander_pick, chip, cross, whole
    )
    far0 = partner(far0_pair, top_bit - 1)
    far1 = partner(far1_pair, top_bit - 2)
    left = shift(left_pair, "wide", 1)
    right = shift(right_pair, "wide", -1)
    stat, acc, upward_t = run_first(plan, queries, upstream, whole, chip, cross)
    stat, acc, wanted = run_far(far2, plan, queries, stat, acc)
    stat, out_t, query_t, far2_term, chip_term, cross_term = run_middle(
        far2, plan, queries, upstream, chip, cross, far0, far1, left, right, stat, acc, upward_t
    )
    back = sides(chip_term, cross_term)
    left_term, right_term, far0_term, far1_term, query_t = run_rest(
        plan, queries, upstream, left, right, far0, far1, stat, query_t
    )

    def own_and_exchange(term, *args):
        return partner(term, top_bit - EXP), run_own(*args)

    def own_alone(term, *args):
        return term, run_own(*args)

    far2_back, (attention, query_grad, key_near, value_near) = lax.cond(
        wanted[0, 0] > 0,
        own_and_exchange,
        own_alone,
        far2_term,
        plan,
        queries,
        upstream,
        whole,
        *back,
        stat,
        out_t,
        query_t,
    )
    key_sum, value_sum = run_first_sum(far2_back, expander_pick, key_near, value_near)
    key_grad, value_grad = run_second_sum(
        expander_pick,
        key_sum,
        value_sum,
        partner(far0_term, top_bit - 1),
        partner(far1_term, top_bit - 2),
        shift(right_term, "wide", 1),
        shift(left_term, "wide", -1),
    )
    return (attention, query_grad, key_grad, value_grad)


def solution(mesh):
    placed = P(("wide", "narrow"), None)
    return jax.shard_map(
        on_device,
        mesh=mesh,
        in_specs=(placed,) * 6,
        out_specs=(placed,) * 4,
        check_vma=False,
    )
```
